32 devices in a mesh: rep: 2 (over x), dp: 4 (over z), mp: 4 (over y, core).
Axes of the slice: x: 2, y: 2, z: 4, core: 2. Of those that a mesh axis runs over, the one named last changes fastest.
Arguments:
- tokens: bfloat16 [3072, 2048], P(('rep', 'dp', 'mp')), may hold values from -6 to 6
- request_ids: int32 [8, 384], P(('rep', 'dp')), may hold values from 0 to 7, never falling along the last dimension, each value on 1 to 192 neighbouring positions
- cache_entries: bfloat16 [4096, 4096], P(('rep', 'dp', 'mp')), may hold values from -250 to 250, as said below
- cached_lengths: int32 [8, 8], replicated, may hold values from 1 to 256, 512 in all within a row
- traded: int32 [4], P('dp'), may hold values from 0 to 1, as said below
- query_weight: bfloat16 [2048, 2048], P(None, 'mp'), may hold values from -0.125 to 0.125
- key_weight: bfloat16 [2048, 2048], P(None, 'mp'), may hold values from -0.125 to 0.125
- value_weight: bfloat16 [2048, 2048], P(None, 'mp'), may hold values from -0.125 to 0.125
- output_weight: bfloat16 [2048, 2048], P('mp'), may hold values from -0.125 to 0.125
- gate_weight: bfloat16 [2048, 8192], P('dp', 'mp'), may hold values from -0.125 to 0.125
- up_weight: bfloat16 [2048, 8192], P('dp', 'mp'), may hold values from -0.125 to 0.125
- down_weight: bfloat16 [2048, 8192], P('dp', 'mp'), may hold values from -0.0625 to 0.0625
Outputs:
- layer_output: bfloat16 [3072, 2048], P(('rep', 'dp', 'mp'))
The draws below stay inside these ranges and needn't reach their ends.
Inputs may be any that keep to these rules, and one draw needn't show every extreme that they name: `request_ids`: each group's row never falls; every request 0 to 7 has 1 to 192 new tokens in each group, some request exactly 192. `cached_lengths`: each row sums to 512; its largest entry is 256. `traded`: exactly 2 entries are 1. `cache_entries`: keys are stored already rotated to their positions; rows of cache group g are g * 512 to (g + 1) * 512 - 1, the requests' prefixes in request order.
All inputs are finite; a program needn't handle non-finite values.
Results may differ from the reference program's by a relative error of at most 0.013.
The reference program's roundings to bfloat16 on the way count: a program that leaves them out, or rounds other values in their place, can miss the bound.
Values may be sent and summed in bfloat16 or wider, within the bound.
No kernel may reach another device: no remote copies, remote signals or barrier semaphores. Data moves between devices by JAX's collectives and lax.ppermute only.
A program may use at most 128 MiB of HBM per device.

```python
import math
import jax
import jax.numpy as jnp
import numpy as np
from jax import lax

D = 2048
HEADS = 16
HEAD_DIM = 128
FF = 8192
TOK_GROUP = 384
CACHE = 512
REQS = 8
PAIRS = 4
GROUPS = 8
TOKENS = 3072
CACHE_ROWS = 4096


def draw_cache_entries(key, part):
    rows = CACHE_ROWS
    base = jax.random.normal(jax.random.fold_in(key, 11), (rows, 2 * D), jnp.float32)
    base = jnp.clip(base, -6.0, 6.0)
    return base.astype(jnp.bfloat16)


def draw_traded(key, part):
    order = jax.random.permutation(jax.random.fold_in(key, 21), PAIRS)
    return (order < PAIRS // 2).astype(jnp.int32)


def steps_of(own_key, extent, shards, low, top_value):
    loudness, own = 1.0, jax.random.fold_in(own_key, 6)
    for axis_at, blocks in shards:
        heights = jnp.exp(jax.random.uniform(jax.random.fold_in(own, axis_at), (blocks,), jnp.float32, low / len(shards), top_value / len(shards)))
        loudness = loudness * jnp.repeat(heights, extent[axis_at] // blocks).reshape([-1 if axis == axis_at else 1 for axis in range(len(extent))])
    return loudness


def length_profile(amount, total, reach, lean):
    weights = [(1 << 20) // math.isqrt(standing ** lean) + 1 for standing in range(2, amount + 1)]
    spare, holding = total - reach - (amount - 1), [1] * (amount - 1)
    while spare > 0:
        movable = [i for i in range(amount - 1) if holding[i] < reach]
        pool, budget = sum([weights[i] for i in movable]), spare
        for i in movable:
            more = min(reach - holding[i], max(1, budget * weights[i] // pool), spare)
            holding[i] = holding[i] + more
            spare = spare - more
    return np.array([reach] + holding)


def ragged_sizes(rng, count, total, most, slope):
    if count == 2:
        one = jax.random.randint(rng, (), max(1, total - most), min(most, total - 1) + 1)
        return jnp.stack([one, total - one])
    lengths = jnp.asarray(length_profile(count, total, most, slope), jnp.int32)
    couples = (count - 1) // 2
    giver, receiver = lengths[1:1 + 2 * couples:2], lengths[2:2 + 2 * couples:2]
    slack = jnp.minimum(giver - 1, most - receiver)
    passed = jax.random.randint(jax.random.fold_in(rng, 1), (couples,), 0, 1 << 20) % (slack + 1)
    lengths = lengths.at[1:1 + 2 * couples:2].set(giver - passed).at[2:2 + 2 * couples:2].set(receiver + passed)
    return lengths[jax.random.permutation(jax.random.fold_in(rng, 2), count)]


def noise(rng, extent, scale, reach, pieces=(), kind=jnp.bfloat16):
    drawn = scale * jax.random.normal(rng, extent, jnp.float32)
    if pieces:
        drawn = drawn * steps_of(rng, extent, pieces, -0.22, 0.18)
    return jnp.clip(drawn, -reach, reach).astype(kind)


def setup_inputs(seed: int = 0) -> dict:
    arg_keys = jax.random.split(jax.random.key(seed), 13)
    tokens = noise(arg_keys[0], (TOKENS, D), 1.0, 6.0, ((0, 32),))
    request_ids = jax.vmap(lambda own: jnp.searchsorted(jnp.cumsum(ragged_sizes(own, REQS, TOK_GROUP, TOK_GROUP // 2, 2)), jnp.arange(TOK_GROUP), side="right"))(jax.random.split(arg_keys[1], GROUPS)).reshape((GROUPS, TOK_GROUP)).astype(jnp.int32)
    cache_entries = draw_cache_entries(jax.random.fold_in(arg_keys[12], 71), 0)
    cached_lengths = jax.vmap(lambda own: ragged_sizes(own, REQS, CACHE, CACHE // 2, 2))(jax.random.split(arg_keys[3], GROUPS)).reshape((GROUPS, REQS)).astype(jnp.int32)
    traded = draw_traded(jax.random.fold_in(arg_keys[12], 71), 0)
    query_weight = noise(arg_keys[5], (D, D), D ** -0.5, 0.125, ((1, 4),))
    key_weight = noise(arg_keys[6], (D, D), D ** -0.5, 0.125, ((1, 4),))
    value_weight = noise(arg_keys[7], (D, D), D ** -0.5, 0.125, ((1, 4),))
    output_weight = noise(arg_keys[8], (D, D), D ** -0.5, 0.125, ((0, 4),))
    gate_weight = noise(arg_keys[9], (D, FF), D ** -0.5, 0.125, ((0, 4), (1, 4)))
    up_weight = noise(arg_keys[10], (D, FF), D ** -0.5, 0.125, ((0, 4), (1, 4)))
    down_weight = noise(arg_keys[11], (D, FF), FF ** -0.5, 0.0625, ((0, 4), (1, 4)))
    return dict(tokens=tokens, request_ids=request_ids, cache_entries=cache_entries, cached_lengths=cached_lengths, traded=traded, query_weight=query_weight, key_weight=key_weight, value_weight=value_weight, output_weight=output_weight, gate_weight=gate_weight, up_weight=up_weight, down_weight=down_weight)


EPSILON = 1e-05
ROPE_BASE = 10000.0

def layer_norm(rows):
    center = rows - lax.optimization_barrier(jnp.mean(rows, axis=-1, keepdims=True))
    spread = lax.optimization_barrier(jnp.mean(center * center, axis=-1, keepdims=True))
    return center * lax.rsqrt(spread + EPSILON)

def request_layout(request_row, length_row, cache_size):
    number = length_row.shape[0]
    labels = jnp.arange(number, dtype=jnp.int32)
    onehot = (request_row[:, None] == labels[None, :]).astype(jnp.int32)
    counts = lax.optimization_barrier(jnp.sum(onehot, axis=0))
    starts = jnp.cumsum(counts) - counts
    token_place = jnp.arange(request_row.shape[0], dtype=jnp.int32)
    positions = lax.optimization_barrier(jnp.sum(onehot * (length_row - starts)[None, :], axis=1)) + token_place
    bounds = jnp.cumsum(length_row)
    cache_place = jnp.arange(cache_size, dtype=jnp.int32)
    owner = lax.optimization_barrier(jnp.sum((cache_place[:, None] >= bounds[None, :]).astype(jnp.int32), axis=1))
    return (positions.astype(jnp.int32), owner.astype(jnp.int32))

def rotate(vectors, positions):
    half = vectors.shape[-1] // 2
    freq = ROPE_BASE ** (-jnp.arange(half, dtype=jnp.float32) / half)
    angle = positions.astype(jnp.float32)[:, None] * freq[None, :]
    cosine = jnp.cos(angle)[:, None, :]
    sine = jnp.sin(angle)[:, None, :]
    first = vectors[..., :half]
    second = vectors[..., half:]
    return jnp.concatenate([first * cosine - second * sine, second * cosine + first * sine], axis=-1)

def attend(query, keys_new, values_new, keys_cache, values_cache, request_row, owner):
    scale = 1.0 / math.sqrt(query.shape[-1])
    keys = jnp.concatenate([keys_cache, keys_new], axis=0)
    values = jnp.concatenate([values_cache, values_new], axis=0)
    scores = jnp.einsum('thd,khd->htk', query.astype(jnp.float32), keys.astype(jnp.float32)) * scale
    count = request_row.shape[0]
    place = jnp.arange(count, dtype=jnp.int32)
    same_cache = owner[None, :] == request_row[:, None]
    same_new = (request_row[None, :] == request_row[:, None]) & (place[None, :] <= place[:, None])
    allowed = jnp.concatenate([same_cache, same_new], axis=1)
    scores = jnp.where(allowed[None], scores, -1e+30)
    top = lax.optimization_barrier(jnp.max(scores, axis=-1, keepdims=True))
    raised = jnp.exp(scores - top)
    total = lax.optimization_barrier(jnp.sum(raised, axis=-1, keepdims=True))
    weights = (raised / total).astype(jnp.bfloat16)
    mixed = jnp.einsum('htk,khd->thd', weights.astype(jnp.float32), values.astype(jnp.float32))
    return mixed.astype(jnp.bfloat16)

def reference(tokens, request_ids, cache_entries, cached_lengths, traded, query_weight, key_weight, value_weight, output_weight, gate_weight, up_weight, down_weight):

    def one_group(group):
        replica = group // PAIRS
        within = group % PAIRS
        source = jnp.where(traded[within] == 1, (1 - replica) * PAIRS + within, group).astype(jnp.int32)
        rows = lax.dynamic_slice_in_dim(tokens, (group * TOK_GROUP).astype(jnp.int32), TOK_GROUP, 0)
        request_row = lax.dynamic_slice_in_dim(request_ids, group.astype(jnp.int32), 1, 0)[0]
        length_row = lax.dynamic_slice_in_dim(cached_lengths, source, 1, 0)[0]
        stored = lax.dynamic_slice_in_dim(cache_entries, (source * CACHE).astype(jnp.int32), CACHE, 0)
        positions, owner = request_layout(request_row, length_row, CACHE)
        normed = layer_norm(rows.astype(jnp.float32)).astype(jnp.bfloat16)
        query = jnp.dot(normed, query_weight, preferred_element_type=jnp.float32).reshape(TOK_GROUP, HEADS, HEAD_DIM)
        query = rotate(query, positions).astype(jnp.bfloat16)
        keys_new = jnp.dot(normed, key_weight, preferred_element_type=jnp.float32).reshape(TOK_GROUP, HEADS, HEAD_DIM)
        keys_new = rotate(keys_new, positions).astype(jnp.bfloat16)
        values_new = jnp.dot(normed, value_weight, preferred_element_type=jnp.float32).astype(jnp.bfloat16).reshape(TOK_GROUP, HEADS, HEAD_DIM)
        keys_cache = stored[:, :D].reshape(CACHE, HEADS, HEAD_DIM)
        values_cache = stored[:, D:].reshape(CACHE, HEADS, HEAD_DIM)
        mixed = attend(query, keys_new, values_new, keys_cache, values_cache, request_row, owner)
        attention = jnp.dot(mixed.reshape(TOK_GROUP, D), output_weight, preferred_element_type=jnp.float32)
        state = (rows.astype(jnp.float32) + attention).astype(jnp.bfloat16)
        normed_two = layer_norm(state.astype(jnp.float32)).astype(jnp.bfloat16)
        gate = jnp.dot(normed_two, gate_weight, preferred_element_type=jnp.float32)
        upward = jnp.dot(normed_two, up_weight, preferred_element_type=jnp.float32)
        activated = (jax.nn.silu(gate) * upward).astype(jnp.bfloat16)
        projected = jnp.dot(activated, down_weight.T, preferred_element_type=jnp.float32)
        return (state.astype(jnp.float32) + projected).astype(jnp.bfloat16)
    outputs = lax.map(one_group, jnp.arange(GROUPS, dtype=jnp.int32))
    return outputs.reshape(TOKENS, D)
```

```python
import math

import jax
import jax.numpy as jnp
from jax import lax
from jax.experimental import pallas as pl
from jax.experimental.pallas import tpu as pltpu
from jax.sharding import PartitionSpec as P

HEAD_DIM = 128
EPSILON = 1e-05
ROPE_BASE = 10000.0
VMEM_LIMIT = 48 * 1024 * 1024
TILE = 256
MASKED = -1e30


def swap(value, axis, mask):
    pairs = [(source, source ^ mask) for source in range(lax.axis_size(axis))]
    return lax.ppermute(value, axis, pairs)


def layer_norm(rows):
    center = rows - jnp.mean(rows, axis=-1, keepdims=True)
    spread = jnp.mean(center * center, axis=-1, keepdims=True)
    return center * lax.rsqrt(spread + EPSILON)


def vmem():
    return pl.BlockSpec(memory_space=pltpu.VMEM)


def smem():
    return pl.BlockSpec(memory_space=pltpu.SMEM)


def anywhere():
    return pl.BlockSpec(memory_space=pl.ANY)


def params():
    return pltpu.CompilerParams(vmem_limit_bytes=VMEM_LIMIT)


def cost(flops, moved, transcendentals=0):
    return pl.CostEstimate(
        flops=flops, bytes_accessed=moved, transcendentals=transcendentals
    )


def project_body(n0, n1, n2, n3, cosine, sine, wq, wk, wv, q_ref, k_ref, v_ref, rows):
    count = n0.shape[0]

    @pl.when(pl.program_id(0) == 0)
    def _():
        for at, part in enumerate((n0, n1, n2, n3)):
            rows[pl.ds(at * count, count), :] = part[...]

    x = rows[...]
    width = wq.shape[1]
    for weight, out, turned in ((wq, q_ref, True), (wk, k_ref, True), (wv, v_ref, False)):
        product = jnp.dot(x, weight[...], preferred_element_type=jnp.float32)
        if not turned:
            out[...] = product.astype(jnp.bfloat16)
            continue
        for at in range(0, width, HEAD_DIM):
            head = product[:, at : at + HEAD_DIM]
            other = pltpu.roll(head, HEAD_DIM // 2, 1)
            out[:, at : at + HEAD_DIM] = (head * cosine[...] + other * sine[...]).astype(
                jnp.bfloat16
            )


def project(parts, cosine, sine, wq, wk, wv):
    count, depth = parts[0].shape
    rows, width = 4 * count, wq.shape[1]
    whole = lambda shape: pl.BlockSpec(shape, lambda i: (0, 0))
    column = pl.BlockSpec((depth, TILE), lambda i: (0, i))
    out = pl.BlockSpec((rows, TILE), lambda i: (0, i))
    shape = jax.ShapeDtypeStruct((rows, width), jnp.bfloat16)
    return pl.pallas_call(
        project_body,
        grid=(width // TILE,),
        in_specs=[whole((count, depth))] * 4 + [whole((rows, HEAD_DIM))] * 2 + [column] * 3,
        out_specs=[out] * 3,
        out_shape=[shape] * 3,
        scratch_shapes=[pltpu.VMEM((rows, depth), jnp.bfloat16)],
        compiler_params=params(),
        cost_estimate=cost(6 * rows * depth * width, 6 * depth * width + 2 * rows * depth),
    )(*parts, cosine, sine, wq, wk, wv)


def attend_body(q, k, v, keep, came, of_row, of_column, wo, near, far, mixed):
    rows = q.shape[0]
    heads = q.shape[1] // HEAD_DIM
    width = q.shape[1]
    cached = of_column.shape[1]
    low, high = of_row[:, 0:1], of_row[:, 1:2]
    first, place = of_row[:, 2:3], of_row[:, 3:4]
    column = of_column[0:1, :]
    fresh = of_column[1:2, :rows]
    on_cached = (column >= low) & (column < high)
    on_fresh = (fresh >= first) & (fresh <= place)
    scale = 1.0 / math.sqrt(HEAD_DIM)
    contract_last = (((1,), (1,)), ((), ()))
    for head in range(heads):
        at = slice(head * HEAD_DIM, (head + 1) * HEAD_DIM)
        after = slice(width + head * HEAD_DIM, width + (head + 1) * HEAD_DIM)
        keys = jnp.concatenate([keep[0, :, at], keep[1, :, at], came[0, :, at], came[1, :, at]])
        values = jnp.concatenate(
            [keep[0, :, after], keep[1, :, after], came[0, :, after], came[1, :, after]]
        )
        query = q[:, at]
        old = lax.dot_general(query, keys, contract_last, preferred_element_type=jnp.float32)
        new = lax.dot_general(query, k[:, at], contract_last, preferred_element_type=jnp.float32)
        old = jnp.where(on_cached, old * scale, MASKED)
        new = jnp.where(on_fresh, new * scale, MASKED)
        top = jnp.maximum(
            jnp.max(old, axis=-1, keepdims=True), jnp.max(new, axis=-1, keepdims=True)
        )
        old = jnp.exp(old - top)
        new = jnp.exp(new - top)
        share = 1.0 / (jnp.sum(old, axis=-1, keepdims=True) + jnp.sum(new, axis=-1, keepdims=True))
        sums = jnp.dot(
            (old * share).astype(jnp.bfloat16), values, preferred_element_type=jnp.float32
        ) + jnp.dot(
            (new * share).astype(jnp.bfloat16), v[:, at], preferred_element_type=jnp.float32
        )
        mixed[:, at] = sums.astype(jnp.bfloat16)
    split_rows(mixed[...], wo, near, far, False)


def split_rows(left, weight, near, far, transposed):
    count = left.shape[0] // 4
    width = near.shape[1]
    for at in range(0, width, TILE):
        if transposed:
            part = sum(
                lax.dot_general(
                    left[:, half * weight.shape[2] : (half + 1) * weight.shape[2]],
                    weight[half, at : at + TILE, :],
                    (((1,), (1,)), ((), ())),
                    preferred_element_type=jnp.float32,
                )
                for half in range(2)
            )
        else:
            part = jnp.dot(left, weight[:, at : at + TILE], preferred_element_type=jnp.float32)
        near[:count, at : at + TILE] = part[:count]
        far[:count, at : at + TILE] = part[count : 2 * count]
        near[count:, at : at + TILE] = part[2 * count : 3 * count]
        far[count:, at : at + TILE] = part[3 * count :]


def attend(q, k, v, keep, came, of_row, of_column, wo):
    rows, width = q.shape
    depth = wo.shape[1]
    shape = jax.ShapeDtypeStruct((rows // 2, depth), jnp.float32)
    cached = of_column.shape[1]
    return pl.pallas_call(
        attend_body,
        in_specs=[vmem()] * 8,
        out_specs=[vmem()] * 2,
        out_shape=[shape] * 2,
        scratch_shapes=[pltpu.VMEM((rows, width), jnp.bfloat16)],
        compiler_params=params(),
        cost_estimate=cost(
            4 * rows * width * (cached + rows) + 2 * rows * width * depth,
            6 * rows * depth,
            rows * (cached + rows) * width // HEAD_DIM,
        ),
    )(q, k, v, keep, came, of_row, of_column, wo)


def gate_up(masks, info, parts, gate, up, mine, other):
    count, depth = parts[0].shape
    rows = 4 * count
    shard, quarter = mine[0].shape[1:]
    pieces = len(mine)

    def body(info_ref, *refs):
        blocks, refs = refs[:4], refs[4:]
        gate_ref, up_ref, refs = refs[0], refs[1], refs[2:]
        sets, refs = (refs[:pieces], refs[pieces : 2 * pieces]), refs[2 * pieces :]
        act_ref, x, held, sems = refs
        own = info_ref[0]
        copies = []
        for half in range(2):
            begin = pl.multiple_of(info_ref[1 + half] * quarter, quarter)
            there = pl.ds(pl.multiple_of(own * shard, shard), shard)
            for which, source in enumerate((gate_ref, up_ref)):
                copies.append(
                    pltpu.make_async_copy(
                        source.at[:, pl.ds(begin, quarter)],
                        held.at[half, which, there, :],
                        sems.at[half, 0, which],
                    )
                )
            for at, mask in enumerate(masks[1:]):
                there = pl.ds(pl.multiple_of((own ^ mask) * shard, shard), shard)
                copies.append(
                    pltpu.make_async_copy(
                        sets[half][at], held.at[half, :, there, :], sems.at[half, at + 1, 0]
                    )
                )
        for copy in copies:
            copy.start()
        for at, block in enumerate(blocks):
            x[pl.ds(at * count, count), :] = block[...]
        for half in range(2):
            for copy in copies[half * (pieces + 2) : (half + 1) * (pieces + 2)]:
                copy.wait()
            for at in range(0, quarter, TILE):
                g = jnp.dot(
                    x[...], held[half, 0, :, at : at + TILE], preferred_element_type=jnp.float32
                )
                u = jnp.dot(
                    x[...], held[half, 1, :, at : at + TILE], preferred_element_type=jnp.float32
                )
                act_ref[:, half * quarter + at : half * quarter + at + TILE] = (
                    g / (1.0 + jnp.exp(-g)) * u
                ).astype(jnp.bfloat16)

    return pl.pallas_call(
        body,
        in_specs=[smem()] + [vmem()] * 4 + [anywhere()] * (2 + 2 * pieces),
        out_specs=vmem(),
        out_shape=jax.ShapeDtypeStruct((rows, 2 * quarter), jnp.bfloat16),
        scratch_shapes=[
            pltpu.VMEM((rows, depth), jnp.bfloat16),
            pltpu.VMEM((2, 2, depth, quarter), jnp.bfloat16),
            pltpu.SemaphoreType.DMA((2, pieces + 1, 2)),
        ],
        compiler_params=params(),
        cost_estimate=cost(8 * rows * depth * quarter, 8 * depth * quarter, 2 * rows * quarter),
    )(info, *parts, gate, up, *mine, *other)


def down_rows(masks, info, act, down, mine, other):
    rows = act.shape[0]
    shard, quarter = mine[0].shape
    pieces = len(mine)
    depth = shard * len(masks)

    def body(info_ref, act_ref, down_ref, *refs):
        sets, refs = (refs[:pieces], refs[pieces : 2 * pieces]), refs[2 * pieces :]
        near, far, held, sems = refs
        own = info_ref[0]
        copies = []
        for half in range(2):
            begin = pl.multiple_of(info_ref[1 + half] * quarter, quarter)
            for at, mask in enumerate(masks):
                there = pl.ds(pl.multiple_of((own ^ mask) * shard, shard), shard)
                source = sets[half][at - 1] if at else down_ref.at[:, pl.ds(begin, quarter)]
                copies.append(
                    pltpu.make_async_copy(source, held.at[half, there, :], sems.at[half, at])
                )
        for copy in copies:
            copy.start()
        for copy in copies:
            copy.wait()
        split_rows(act_ref[...], held, near, far, True)

    shape = jax.ShapeDtypeStruct((rows // 2, depth), jnp.float32)
    return pl.pallas_call(
        body,
        in_specs=[smem(), vmem()] + [anywhere()] * (1 + 2 * pieces),
        out_specs=[vmem()] * 2,
        out_shape=[shape] * 2,
        scratch_shapes=[
            pltpu.VMEM((2, depth, quarter), jnp.bfloat16),
            pltpu.SemaphoreType.DMA((2, pieces + 1)),
        ],
        compiler_params=params(),
        cost_estimate=cost(4 * rows * depth * quarter, 4 * depth * quarter + 4 * rows * depth),
    )(info, act, down, *mine, *other)


def gather_rows(rows):
    across = swap(rows, "mp", 2)
    return [rows, swap(rows, "mp", 1), across, swap(across, "mp", 1)]


def reduce_rows(near, far):
    count = near.shape[0] // 2
    came = swap(far, "mp", 1)
    sent = (near[count:] + came[count:]).astype(jnp.bfloat16)
    return near[:count] + came[:count] + swap(sent, "mp", 2).astype(jnp.float32)


def spread_pieces(own, leaving, pair, bits):
    pieces = {0: own, pair: swap(leaving, "dp", pair)}
    for bit in bits:
        pieces.update({mask ^ bit: swap(piece, "dp", bit) for mask, piece in list(pieces.items())})
    return pieces


def row_facts(request_row, length_row, member, cache_size):
    count = request_row.shape[0]
    number = length_row.shape[0]
    labels = jnp.arange(number, dtype=jnp.int32)
    onehot = (request_row[:, None] == labels[None, :]).astype(jnp.int32)
    counts = jnp.sum(onehot, axis=0)
    below = labels[:, None] < labels[None, :]
    starts = jnp.sum(jnp.where(below, counts[:, None], 0), axis=0)
    begins = jnp.sum(jnp.where(below, length_row[:, None], 0), axis=0)

    def blocks(size, order):
        step = jnp.arange(size // 4, dtype=jnp.int32)
        return jnp.concatenate([(member ^ mask) * (size // 4) + step for mask in order])

    place = blocks(count, (0, 1, 2, 3))
    request = jnp.concatenate(
        [
            lax.dynamic_slice_in_dim(request_row, (member ^ mask) * (count // 4), count // 4, 0)
            for mask in range(4)
        ]
    )
    onehot = (request[:, None] == labels[None, :]).astype(jnp.int32)
    first = jnp.sum(onehot * starts[None, :], axis=1)
    length = jnp.sum(onehot * length_row[None, :], axis=1)
    low = jnp.sum(onehot * begins[None, :], axis=1)
    positions = length + place - first
    of_row = jnp.stack([low, low + length, first, place], axis=1)
    cached = blocks(cache_size, (0, 2, 1, 3))
    of_column = jnp.stack([cached, jnp.pad(place, (0, cache_size - count))])
    return positions, of_row, of_column


def local(
    tokens,
    request_ids,
    cache_entries,
    cached_lengths,
    traded,
    query_weight,
    key_weight,
    value_weight,
    output_weight,
    gate_weight,
    up_weight,
    down_weight,
):
    replica = lax.axis_index("rep")
    within = lax.axis_index("dp")
    member = lax.axis_index("mp")
    planes = lax.axis_size("dp")
    group = replica * planes + within
    moved_here = traded[0] == 1
    source = jnp.where(moved_here, (1 - replica) * planes + within, group)
    length_row = lax.dynamic_slice_in_dim(cached_lengths, source, 1, 0)[0]

    normed = layer_norm(tokens.astype(jnp.float32)).astype(jnp.bfloat16)
    parts = gather_rows(normed)

    held, width = cache_entries.shape
    chip, core = member // 2, member % 2
    entries = cache_entries.reshape(held, 2, 2, 2, width // 8)
    near = lax.dynamic_slice_in_dim(entries, chip, 1, 2)[:, :, 0]
    far = lax.dynamic_slice_in_dim(entries, 1 - chip, 1, 2)[:, :, 0]
    near_came = swap(near, "rep", 1)
    far = swap(far, "mp", 2)
    far_came = swap(far, "rep", 1)
    near = jnp.where(moved_here, near_came, near)
    far = jnp.where(moved_here, far_came, far)

    def of_core(which):
        return jnp.stack(
            [
                lax.dynamic_slice_in_dim(rows, which, 1, 2).reshape(held, width // 4)
                for rows in (near, far)
            ]
        )

    keep = of_core(core)
    came = swap(of_core(1 - core), "mp", 1)

    pair = planes // 2
    bits = [1 << at for at in range(planes.bit_length() - 1) if 1 << at != pair]
    half = (within // pair) % 2
    quarter = gate_weight.shape[1] // 4
    index_mine, index_other = 2 * half + replica, 2 * half + 1 - replica
    index_leaving = 2 * (1 - half) + replica

    def cut(weight, index):
        return lax.dynamic_slice_in_dim(weight, index * quarter, quarter, 1)

    def gate_and_up(index):
        return jnp.stack([cut(gate_weight, index), cut(up_weight, index)])

    wide = spread_pieces(gate_and_up(index_mine), gate_and_up(index_leaving), pair, bits)
    masks = list(wide)
    wide_mine = [wide[mask] for mask in masks[1:]]
    wide_other = [swap(piece, "rep", 1) for piece in wide_mine]
    back = spread_pieces(cut(down_weight, index_mine), cut(down_weight, index_leaving), pair, bits)
    back_mine = [back[mask] for mask in masks[1:]]
    back_other = [swap(piece, "rep", 1) for piece in back_mine]
    info = jnp.stack([within, index_mine, index_other]).astype(jnp.int32)

    positions, of_row, of_column = row_facts(request_ids[0], length_row, member, 4 * held)
    half_dim = HEAD_DIM // 2
    freq = ROPE_BASE ** (-jnp.arange(half_dim, dtype=jnp.float32) / half_dim)
    angle = positions.astype(jnp.float32)[:, None] * freq[None, :]
    cosine, sine = jnp.cos(angle), jnp.sin(angle)
    cosine = jnp.concatenate([cosine, cosine], axis=1)
    sine = jnp.concatenate([-sine, sine], axis=1)
    q, k, v = project(parts, cosine, sine, query_weight, key_weight, value_weight)
    own_sum = reduce_rows(*attend(q, k, v, keep, came, of_row, of_column, output_weight))
    state_own = (tokens.astype(jnp.float32) + own_sum).astype(jnp.bfloat16)
    normed_own = layer_norm(state_own.astype(jnp.float32)).astype(jnp.bfloat16)

    rows_pair = gather_rows(swap(normed_own, "dp", pair))
    rows_own = gather_rows(normed_own)
    act_own = gate_up(masks, info, rows_own, gate_weight, up_weight, wide_mine, wide_other)
    act_pair = gate_up(masks, info, rows_pair, gate_weight, up_weight, wide_mine, wide_other)
    pair_sum = reduce_rows(*down_rows(masks, info, act_pair, down_weight, back_mine, back_other))
    own_sum = reduce_rows(*down_rows(masks, info, act_own, down_weight, back_mine, back_other))
    came_sum = swap(pair_sum.astype(jnp.bfloat16), "dp", pair).astype(jnp.float32)
    return (state_own.astype(jnp.float32) + (own_sum + came_sum)).astype(jnp.bfloat16)


def solution(mesh):
    in_specs = (
        P(("rep", "dp", "mp"), None),
        P(("rep", "dp"), None),
        P(("rep", "dp", "mp"), None),
        P(),
        P("dp"),
        P(None, "mp"),
        P(None, "mp"),
        P(None, "mp"),
        P("mp", None),
        P("dp", "mp"),
        P("dp", "mp"),
        P("dp", "mp"),
    )
    out_specs = P(("rep", "dp", "mp"), None)
    return jax.shard_map(local, mesh=mesh, in_specs=in_specs, out_specs=out_specs, check_vma=False)
```

```python
import math

import jax
import jax.numpy as jnp
from jax import lax
from jax.experimental import pallas as pl
from jax.experimental.pallas import tpu as pltpu
from jax.sharding import PartitionSpec as P

HEAD_DIM = 128
EPSILON = 1e-05
ROPE_BASE = 10000.0
VMEM_LIMIT = 48 * 1024 * 1024
TILE = 256
MASKED = -1e30
Z_APART = 2
X_APART = 1


def swap(value, axis, mask):
    pairs = [(source, source ^ mask) for source in range(lax.axis_size(axis))]
    return lax.ppermute(value, axis, pairs)


def layer_norm(rows):
    center = rows - jnp.mean(rows, axis=-1, keepdims=True)
    spread = jnp.mean(center * center, axis=-1, keepdims=True)
    return center * lax.rsqrt(spread + EPSILON)


def vmem():
    return pl.BlockSpec(memory_space=pltpu.VMEM)


def smem():
    return pl.BlockSpec(memory_space=pltpu.SMEM)


def anywhere():
    return pl.BlockSpec(memory_space=pl.ANY)


def params():
    return pltpu.CompilerParams(vmem_limit_bytes=VMEM_LIMIT)


def cost(flops, moved, transcendentals=0):
    return pl.CostEstimate(
        flops=flops, bytes_accessed=moved, transcendentals=transcendentals
    )


def prepare_body(info, tokens, entries, normed, near, far):
    normed[...] = layer_norm(tokens[...].astype(jnp.float32)).astype(jnp.bfloat16)
    half = near.shape[1] // 2
    for out, chip in ((near, info[0]), (far, 1 - info[0])):
        begin = pl.multiple_of(chip * half, half)
        out[:, :half] = entries[:, pl.ds(begin, half)]
        out[:, half:] = entries[:, pl.ds(2 * half + begin, half)]


def prepare(info, tokens, entries):
    part = jax.ShapeDtypeStruct((entries.shape[0], entries.shape[1] // 2), jnp.bfloat16)
    return pl.pallas_call(
        prepare_body,
        in_specs=[smem(), vmem(), vmem()],
        out_specs=[vmem()] * 3,
        out_shape=[jax.ShapeDtypeStruct(tokens.shape, jnp.bfloat16), part, part],
        compiler_params=params(),
        cost_estimate=cost(10 * tokens.size, 4 * tokens.size + 4 * entries.size),
    )(info, tokens, entries)


def cut_body(info, gate, up, down, *refs):
    outs, sems = refs[:-1], refs[-1]
    quarter = outs[0].shape[1]
    copies = []
    for at, out in enumerate(outs):
        begin = pl.multiple_of(info[1 + at // 3] * quarter, quarter)
        source = (gate, up, down)[at % 3].at[:, pl.ds(begin, quarter)]
        copies.append(pltpu.make_async_copy(source, out, sems.at[at]))
    for copy in copies:
        copy.start()
    for copy in copies:
        copy.wait()


def cut(info, *weights):
    rows, columns = weights[0].shape
    shape = jax.ShapeDtypeStruct((rows, columns // 4), jnp.bfloat16)
    return pl.pallas_call(
        cut_body,
        in_specs=[smem()] + [anywhere()] * 3,
        out_specs=[anywhere()] * 6,
        out_shape=[shape] * 6,
        scratch_shapes=[pltpu.SemaphoreType.DMA((6,))],
        compiler_params=params(),
        cost_estimate=cost(0, 6 * rows * columns),
    )(info, *weights)


def pick_body(info, near, near_came, far, far_came, keep, send):
    quarter = keep.shape[2] // 2
    moved = info[0] == 1

    def fill(sources):
        for at, source in enumerate(sources):
            for out, core in ((keep, info[1]), (send, 1 - info[1])):
                begin = pl.multiple_of(core * quarter, quarter)
                out[at, :, :quarter] = source[:, pl.ds(begin, quarter)]
                out[at, :, quarter:] = source[:, pl.ds(2 * quarter + begin, quarter)]

    @pl.when(moved)
    def _():
        fill((near_came, far_came))

    @pl.when(jnp.logical_not(moved))
    def _():
        fill((near, far))


def pick(info, near, near_came, far, far_came):
    shape = jax.ShapeDtypeStruct((2, near.shape[0], near.shape[1] // 2), jnp.bfloat16)
    return pl.pallas_call(
        pick_body,
        in_specs=[smem()] + [vmem()] * 4,
        out_specs=[vmem()] * 2,
        out_shape=[shape] * 2,
        compiler_params=params(),
        cost_estimate=cost(0, 12 * near.size),
    )(info, near, near_came, far, far_came)


def project_body(n0, n1, n2, n3, cosine, sine, wq, wk, wv, q_ref, k_ref, v_ref, rows):
    count = n0.shape[0]

    @pl.when(pl.program_id(0) == 0)
    def _():
        for at, part in enumerate((n0, n1, n2, n3)):
            rows[pl.ds(at * count, count), :] = part[...]

    x = rows[...]
    width = wq.shape[1]
    for weight, out, turned in ((wq, q_ref, True), (wk, k_ref, True), (wv, v_ref, False)):
        product = jnp.dot(x, weight[...], preferred_element_type=jnp.float32)
        if not turned:
            out[...] = product.astype(jnp.bfloat16)
            continue
        for at in range(0, width, HEAD_DIM):
            head = product[:, at : at + HEAD_DIM]
            other = pltpu.roll(head, HEAD_DIM // 2, 1)
            out[:, at : at + HEAD_DIM] = (head * cosine[...] + other * sine[...]).astype(
                jnp.bfloat16
            )


def project(parts, cosine, sine, wq, wk, wv):
    count, depth = parts[0].shape
    rows, width = 4 * count, wq.shape[1]
    whole = lambda shape: pl.BlockSpec(shape, lambda i: (0, 0))
    column = pl.BlockSpec((depth, TILE), lambda i: (0, i))
    out = pl.BlockSpec((rows, TILE), lambda i: (0, i))
    shape = jax.ShapeDtypeStruct((rows, width), jnp.bfloat16)
    return pl.pallas_call(
        project_body,
        grid=(width // TILE,),
        in_specs=[whole((count, depth))] * 4 + [whole((rows, HEAD_DIM))] * 2 + [column] * 3,
        out_specs=[out] * 3,
        out_shape=[shape] * 3,
        scratch_shapes=[pltpu.VMEM((rows, depth), jnp.bfloat16)],
        compiler_params=params(),
        cost_estimate=cost(6 * rows * depth * width, 6 * depth * width + 2 * rows * depth),
    )(*parts, cosine, sine, wq, wk, wv)


def attend_body(q, k, v, keep, came, of_row, of_column, wo, near, far, mixed):
    rows = q.shape[0]
    heads = q.shape[1] // HEAD_DIM
    width = q.shape[1]
    cached = of_column.shape[1]
    low, high = of_row[:, 0:1], of_row[:, 1:2]
    first, place = of_row[:, 2:3], of_row[:, 3:4]
    column = of_column[0:1, :]
    fresh = of_column[1:2, :rows]
    on_cached = (column >= low) & (column < high)
    on_fresh = (fresh >= first) & (fresh <= place)
    scale = 1.0 / math.sqrt(HEAD_DIM)
    contract_last = (((1,), (1,)), ((), ()))
    for head in range(heads):
        at = slice(head * HEAD_DIM, (head + 1) * HEAD_DIM)
        after = slice(width + head * HEAD_DIM, width + (head + 1) * HEAD_DIM)
        keys = jnp.concatenate([keep[0, :, at], keep[1, :, at], came[0, :, at], came[1, :, at]])
        values = jnp.concatenate(
            [keep[0, :, after], keep[1, :, after], came[0, :, after], came[1, :, after]]
        )
        query = q[:, at]
        old = lax.dot_general(query, keys, contract_last, preferred_element_type=jnp.float32)
        new = lax.dot_general(query, k[:, at], contract_last, preferred_element_type=jnp.float32)
        old = jnp.where(on_cached, old * scale, MASKED)
        new = jnp.where(on_fresh, new * scale, MASKED)
        top = jnp.maximum(
            jnp.max(old, axis=-1, keepdims=True), jnp.max(new, axis=-1, keepdims=True)
        )
        old = jnp.exp(old - top)
        new = jnp.exp(new - top)
        share = 1.0 / (jnp.sum(old, axis=-1, keepdims=True) + jnp.sum(new, axis=-1, keepdims=True))
        sums = jnp.dot(
            (old * share).astype(jnp.bfloat16), values, preferred_element_type=jnp.float32
        ) + jnp.dot(
            (new * share).astype(jnp.bfloat16), v[:, at], preferred_element_type=jnp.float32
        )
        mixed[:, at] = sums.astype(jnp.bfloat16)
    split_rows(mixed[...], wo, near, far, False)


def split_rows(left, weight, near, far, transposed):
    count = left.shape[0] // 4
    width = near.shape[1]
    for at in range(0, width, TILE):
        if transposed:
            part = sum(
                lax.dot_general(
                    left[:, half * weight.shape[2] : (half + 1) * weight.shape[2]],
                    weight[half, at : at + TILE, :],
                    (((1,), (1,)), ((), ())),
                    preferred_element_type=jnp.float32,
                )
                for half in range(2)
            )
        else:
            part = jnp.dot(left, weight[:, at : at + TILE], preferred_element_type=jnp.float32)
        near[:count, at : at + TILE] = part[:count]
        far[:count, at : at + TILE] = part[count : 2 * count]
        near[count:, at : at + TILE] = part[2 * count : 3 * count]
        far[count:, at : at + TILE] = part[3 * count :]


def attend(q, k, v, keep, came, of_row, of_column, wo):
    rows, width = q.shape
    depth = wo.shape[1]
    shape = jax.ShapeDtypeStruct((rows // 2, depth), jnp.float32)
    cached = of_column.shape[1]
    return pl.pallas_call(
        attend_body,
        in_specs=[vmem()] * 8,
        out_specs=[vmem()] * 2,
        out_shape=[shape] * 2,
        scratch_shapes=[pltpu.VMEM((rows, width), jnp.bfloat16)],
        compiler_params=params(),
        cost_estimate=cost(
            4 * rows * width * (cached + rows) + 2 * rows * width * depth,
            6 * rows * depth,
            rows * (cached + rows) * width // HEAD_DIM,
        ),
    )(q, k, v, keep, came, of_row, of_column, wo)


def gate_up(masks, info, parts, gate, up, mine, other):
    count, depth = parts[0].shape
    rows = 4 * count
    shard, quarter = mine[0][0].shape
    pieces = len(mine[0])

    def body(info_ref, *refs):
        blocks, refs = refs[:4], refs[4:]
        wholes, refs = refs[:2], refs[2:]
        sets, refs = refs[: 4 * pieces], refs[4 * pieces :]
        act_ref, x, held, sems = refs
        own = info_ref[0]
        copies = []
        for half in range(2):
            begin = pl.multiple_of(info_ref[1 + half] * quarter, quarter)
            for which in range(2):
                for at, mask in enumerate(masks):
                    there = pl.ds(pl.multiple_of((own ^ mask) * shard, shard), shard)
                    if at:
                        source = sets[(2 * half + which) * pieces + at - 1]
                    else:
                        source = wholes[which].at[:, pl.ds(begin, quarter)]
                    copies.append(
                        pltpu.make_async_copy(
                            source, held.at[half, which, there, :], sems.at[half, which, at]
                        )
                    )
        for copy in copies:
            copy.start()
        for at, block in enumerate(blocks):
            x[pl.ds(at * count, count), :] = block[...]
        for half in range(2):
            for copy in copies[2 * half * (pieces + 1) : 2 * (half + 1) * (pieces + 1)]:
                copy.wait()
            for at in range(0, quarter, TILE):
                g = jnp.dot(
                    x[...], held[half, 0, :, at : at + TILE], preferred_element_type=jnp.float32
                )
                u = jnp.dot(
                    x[...], held[half, 1, :, at : at + TILE], preferred_element_type=jnp.float32
                )
                act_ref[:, half * quarter + at : half * quarter + at + TILE] = (
                    g / (1.0 + jnp.exp(-g)) * u
                ).astype(jnp.bfloat16)

    return pl.pallas_call(
        body,
        in_specs=[smem()] + [vmem()] * 4 + [anywhere()] * (2 + 4 * pieces),
        out_specs=vmem(),
        out_shape=jax.ShapeDtypeStruct((rows, 2 * quarter), jnp.bfloat16),
        scratch_shapes=[
            pltpu.VMEM((rows, depth), jnp.bfloat16),
            pltpu.VMEM((2, 2, depth, quarter), jnp.bfloat16),
            pltpu.SemaphoreType.DMA((2, 2, pieces + 1)),
        ],
        compiler_params=params(),
        cost_estimate=cost(8 * rows * depth * quarter, 8 * depth * quarter, 2 * rows * quarter),
    )(info, *parts, gate, up, *mine[0], *mine[1], *other[0], *other[1])


def down_rows(masks, info, act, down, mine, other):
    rows = act.shape[0]
    shard, quarter = mine[0].shape
    pieces = len(mine)
    depth = shard * len(masks)

    def body(info_ref, act_ref, down_ref, *refs):
        sets, refs = (refs[:pieces], refs[pieces : 2 * pieces]), refs[2 * pieces :]
        near, far, held, sems = refs
        own = info_ref[0]
        copies = []
        for half in range(2):
            begin = pl.multiple_of(info_ref[1 + half] * quarter, quarter)
            for at, mask in enumerate(masks):
                there = pl.ds(pl.multiple_of((own ^ mask) * shard, shard), shard)
                source = sets[half][at - 1] if at else down_ref.at[:, pl.ds(begin, quarter)]
                copies.append(
                    pltpu.make_async_copy(source, held.at[half, there, :], sems.at[half, at])
                )
        for copy in copies:
            copy.start()
        for copy in copies:
            copy.wait()
        split_rows(act_ref[...], held, near, far, True)

    shape = jax.ShapeDtypeStruct((rows // 2, depth), jnp.float32)
    return pl.pallas_call(
        body,
        in_specs=[smem(), vmem()] + [anywhere()] * (1 + 2 * pieces),
        out_specs=[vmem()] * 2,
        out_shape=[shape] * 2,
        scratch_shapes=[
            pltpu.VMEM((2, depth, quarter), jnp.bfloat16),
            pltpu.SemaphoreType.DMA((2, pieces + 1)),
        ],
        compiler_params=params(),
        cost_estimate=cost(4 * rows * depth * quarter, 4 * depth * quarter + 4 * rows * depth),
    )(info, act, down, *mine, *other)


def gather_rows(rows):
    across = swap(rows, "mp", 2)
    return [rows, swap(rows, "mp", 1), across, swap(across, "mp", 1)]


def reduce_rows(near, far):
    count = near.shape[0] // 2
    came = swap(far, "mp", 1)
    sent = (near[count:] + came[count:]).astype(jnp.bfloat16)
    return near[:count] + came[:count] + swap(sent, "mp", 2).astype(jnp.float32)


def after(value, *earlier):
    return lax.optimization_barrier((value,) + earlier)[0] if earlier else value


def queue(transfers, apart):
    done = []
    for transfer in transfers:
        done.append(transfer(*done[-apart:][:1]) if len(done) >= apart else transfer())
    return done


def spread_weights(mine, leaving, pair, bits, first):
    steps = [[], [(0, pair)], []]
    for start, step in ((0, steps[0]), (pair, steps[2])):
        known = [start]
        for bit in bits:
            step += [(mask, bit) for mask in known]
            known += [mask ^ bit for mask in known]
    held = [{0: piece} for piece in mine]

    def over_planes(weight, mask, bit):
        def transfer(*earlier):
            piece = leaving[weight] if bit == pair else held[weight][mask]
            held[weight][mask ^ bit] = swap(after(piece, *earlier), "dp", bit)
            return held[weight][mask ^ bit]

        return transfer

    order = [(0, 0), (0, 1), (1, 0), (1, 1), (0, 2), (2, 1), (1, 2), (2, 0), (2, 2)]
    queue([over_planes(w, *step) for w, kind in order for step in steps[kind]], Z_APART)
    other = [{} for _ in mine]

    def over_replicas(weight, mask):
        def transfer(*earlier):
            other[weight][mask] = swap(after(held[weight][mask], *earlier), "rep", 1)
            return other[weight][mask]

        return transfer

    order = [(0, 0), (0, 1), (1, 0), (1, 1), (0, 2), (1, 2), (2, 0), (2, 1), (2, 2)]
    line = [lambda *_: first]
    queue(line + [over_replicas(w, m ^ b) for w, kind in order for m, b in steps[kind]], X_APART)
    masks = [0] + [mask ^ bit for step in steps for mask, bit in step]
    pieces = lambda sets: [[part[mask] for mask in masks[1:]] for part in sets]
    return masks, pieces(held), pieces(other)


def row_facts(request_row, length_row, member, cache_size):
    count = request_row.shape[0]
    number = length_row.shape[0]
    labels = jnp.arange(number, dtype=jnp.int32)
    onehot = (request_row[:, None] == labels[None, :]).astype(jnp.int32)
    counts = jnp.sum(onehot, axis=0)
    below = labels[:, None] < labels[None, :]
    starts = jnp.sum(jnp.where(below, counts[:, None], 0), axis=0)
    begins = jnp.sum(jnp.where(below, length_row[:, None], 0), axis=0)

    def blocks(size, order):
        step = jnp.arange(size // 4, dtype=jnp.int32)
        return jnp.concatenate([(member ^ mask) * (size // 4) + step for mask in order])

    place = blocks(count, (0, 1, 2, 3))
    request = jnp.concatenate(
        [
            lax.dynamic_slice_in_dim(request_row, (member ^ mask) * (count // 4), count // 4, 0)
            for mask in range(4)
        ]
    )
    onehot = (request[:, None] == labels[None, :]).astype(jnp.int32)
    first = jnp.sum(onehot * starts[None, :], axis=1)
    length = jnp.sum(onehot * length_row[None, :], axis=1)
    low = jnp.sum(onehot * begins[None, :], axis=1)
    positions = length + place - first
    of_row = jnp.stack([low, low + length, first, place], axis=1)
    cached = blocks(cache_size, (0, 2, 1, 3))
    of_column = jnp.stack([cached, jnp.pad(place, (0, cache_size - count))])
    return positions, of_row, of_column


def local(
    tokens,
    request_ids,
    cache_entries,
    cached_lengths,
    traded,
    query_weight,
    key_weight,
    value_weight,
    output_weight,
    gate_weight,
    up_weight,
    down_weight,
):
    replica = lax.axis_index("rep")
    within = lax.axis_index("dp")
    member = lax.axis_index("mp")
    planes = lax.axis_size("dp")
    group = replica * planes + within
    moved_here = traded[0] == 1
    source = jnp.where(moved_here, (1 - replica) * planes + within, group)
    length_row = lax.dynamic_slice_in_dim(cached_lengths, source, 1, 0)[0]

    chip, core = member // 2, member % 2
    normed, near, far = prepare(chip[None].astype(jnp.int32), tokens, cache_entries)
    near_came = swap(near, "rep", 1)
    far = swap(far, "mp", 2)
    parts = gather_rows(normed)
    far_came = swap(far, "rep", 1)
    choice = jnp.stack([traded[0], core]).astype(jnp.int32)
    keep, came = pick(choice, near, near_came, far, far_came)
    came = swap(came, "mp", 1)

    pair = planes // 2
    bits = [1 << at for at in range(planes.bit_length() - 1) if 1 << at != pair]
    half = (within // pair) % 2
    index_mine, index_other = 2 * half + replica, 2 * half + 1 - replica
    index_leaving = 2 * (1 - half) + replica
    info = jnp.stack([within, index_mine, index_other, index_leaving]).astype(jnp.int32)
    cuts = cut(info[jnp.array([0, 1, 3])], gate_weight, up_weight, down_weight)
    masks, mine, other = spread_weights(cuts[:3], cuts[3:], pair, bits, far_came)

    positions, of_row, of_column = row_facts(request_ids[0], length_row, member, 4 * cache_entries.shape[0])
    half_dim = HEAD_DIM // 2
    freq = ROPE_BASE ** (-jnp.arange(half_dim, dtype=jnp.float32) / half_dim)
    angle = positions.astype(jnp.float32)[:, None] * freq[None, :]
    cosine, sine = jnp.cos(angle), jnp.sin(angle)
    cosine = jnp.concatenate([cosine, cosine], axis=1)
    sine = jnp.concatenate([-sine, sine], axis=1)
    q, k, v = project(parts, cosine, sine, query_weight, key_weight, value_weight)
    own_sum = reduce_rows(*attend(q, k, v, keep, came, of_row, of_column, output_weight))
    state_own = (tokens.astype(jnp.float32) + own_sum).astype(jnp.bfloat16)
    normed_own = layer_norm(state_own.astype(jnp.float32)).astype(jnp.bfloat16)

    rows_pair = gather_rows(swap(normed_own, "dp", pair))
    rows_own = gather_rows(normed_own)
    act_own = gate_up(masks, info, rows_own, gate_weight, up_weight, mine[:2], other[:2])
    act_pair = gate_up(masks, info, rows_pair, gate_weight, up_weight, mine[:2], other[:2])
    pair_sum = reduce_rows(*down_rows(masks, info, act_pair, down_weight, mine[2], other[2]))
    own_sum = reduce_rows(*down_rows(masks, info, act_own, down_weight, mine[2], other[2]))
    came_sum = swap(pair_sum.astype(jnp.bfloat16), "dp", pair).astype(jnp.float32)
    return (state_own.astype(jnp.float32) + (own_sum + came_sum)).astype(jnp.bfloat16)


def solution(mesh):
    in_specs = (
        P(("rep", "dp", "mp"), None),
        P(("rep", "dp"), None),
        P(("rep", "dp", "mp"), None),
        P(),
        P("dp"),
        P(None, "mp"),
        P(None, "mp"),
        P(None, "mp"),
        P("mp", None),
        P("dp", "mp"),
        P("dp", "mp"),
        P("dp", "mp"),
    )
    out_specs = P(("rep", "dp", "mp"), None)
    return jax.shard_map(local, mesh=mesh, in_specs=in_specs, out_specs=out_specs, check_vma=False)
```

```python
import math

import jax
import jax.numpy as jnp
import numpy as np
from jax import lax
from jax.experimental import pallas as pl
from jax.experimental.pallas import tpu as pltpu
from jax.sharding import PartitionSpec as P

HEAD_DIM = 128
EPSILON = 1e-05
ROPE_BASE = 10000.0
VMEM_LIMIT = 60 * 1024 * 1024
TILE = 256
MASKED = -1e30
FAR_PARTS = 4
MEMBER, WITHIN, MINE, LEAVING, SOURCE = range(5)


def swap(value, axis, mask):
    pairs = [(source, source ^ mask) for source in range(lax.axis_size(axis))]
    return lax.ppermute(value, axis, pairs)


def layer_norm(rows):
    center = rows - jnp.mean(rows, axis=-1, keepdims=True)
    spread = jnp.mean(center * center, axis=-1, keepdims=True)
    return center * lax.rsqrt(spread + EPSILON)


def vmem():
    return pl.BlockSpec(memory_space=pltpu.VMEM)


def smem():
    return pl.BlockSpec(memory_space=pltpu.SMEM)


def anywhere():
    return pl.BlockSpec(memory_space=pl.ANY)


def params():
    return pltpu.CompilerParams(vmem_limit_bytes=VMEM_LIMIT)


def cost(gate=True):
    return pl.CostEstimate(flops=10**11 if gate else 0, bytes_accessed=0, transcendentals=0)


def prepare(info, tokens, entries, *weights):
    rows, columns = entries.shape
    stack, depth, width = len(weights), weights[0].shape[0], weights[0].shape[1] // 4

    def body(info_ref, token_ref, entry_ref, *refs):
        sources, normed, blocks = refs[:stack], refs[stack], refs[stack + 1 : stack + 5]
        outs, sems = refs[stack + 5 : -1], refs[-1]
        copies = cut_copies(info_ref, sources, outs, sems)
        part = blocks[0].shape[1] // 2
        for mask, out in enumerate(blocks):
            begin = pl.multiple_of((info_ref[MEMBER] ^ mask) * part, part)
            out[:, :part] = entry_ref[:, pl.ds(begin, part)]
            out[:, part:] = entry_ref[:, pl.ds(4 * part + begin, part)]
        normed[...] = layer_norm(token_ref[...].astype(jnp.float32)).astype(jnp.bfloat16)
        for copy in copies:
            copy.wait()

    return pl.pallas_call(
        body,
        in_specs=[smem(), vmem(), vmem()] + [anywhere()] * stack,
        out_specs=[vmem()] * 7,
        out_shape=[jax.ShapeDtypeStruct(tokens.shape, jnp.bfloat16)]
        + [jax.ShapeDtypeStruct((rows, columns // 4), jnp.bfloat16)] * 4
        + [jax.ShapeDtypeStruct((stack * depth, width), jnp.bfloat16)] * 2,
        scratch_shapes=[pltpu.SemaphoreType.DMA((2, stack))],
        compiler_params=params(),
        cost_estimate=cost(False),
    )(info, tokens, entries, *weights)


def cut_copies(info, sources, outs, sems):
    rows = sources[0].shape[0]
    width = outs[0].shape[1]
    copies = []
    for at, out in enumerate(outs):
        there = pl.ds(pl.multiple_of(info[(LEAVING, MINE)[at]] * width, width), width)
        for which, source in enumerate(sources):
            place = out.at[pl.ds(which * rows, rows), :]
            copies.append(pltpu.make_async_copy(source.at[:, there], place, sems.at[at, which]))
    for copy in copies:
        copy.start()
    return copies


def cut(info, *weights):
    rows, columns = weights[0].shape
    width = columns // 4
    count, stack = 2, len(weights)

    def body(info_ref, *refs):
        for copy in cut_copies(info_ref, refs[:stack], refs[stack:-1], refs[-1]):
            copy.wait()

    return pl.pallas_call(
        body,
        in_specs=[smem()] + [anywhere()] * stack,
        out_specs=[vmem()] * count,
        out_shape=[jax.ShapeDtypeStruct((stack * rows, width), jnp.bfloat16)] * count,
        scratch_shapes=[pltpu.SemaphoreType.DMA((count, stack))],
        compiler_params=params(),
        cost_estimate=cost(False),
    )(info, *weights)


def project_body(n0, n1, n2, n3, cosine, sine, wq, wk, wv, q_ref, k_ref, v_ref, rows):
    count = n0.shape[0]

    @pl.when(pl.program_id(0) == 0)
    def _():
        for at, part in enumerate((n0, n1, n2, n3)):
            rows[pl.ds(at * count, count), :] = part[...]

    x = rows[...]
    width = wq.shape[1]
    for weight, out, turned in ((wq, q_ref, True), (wk, k_ref, True), (wv, v_ref, False)):
        product = jnp.dot(x, weight[...], preferred_element_type=jnp.float32)
        if not turned:
            out[...] = product.astype(jnp.bfloat16)
            continue
        for at in range(0, width, HEAD_DIM):
            head = product[:, at : at + HEAD_DIM]
            other = pltpu.roll(head, HEAD_DIM // 2, 1)
            out[:, at : at + HEAD_DIM] = (head * cosine[...] + other * sine[...]).astype(
                jnp.bfloat16
            )


def project(parts, cosine, sine, wq, wk, wv):
    count, depth = parts[0].shape
    rows, width = 4 * count, wq.shape[1]
    whole = lambda shape: pl.BlockSpec(shape, lambda i: (0, 0))
    column = pl.BlockSpec((depth, TILE), lambda i: (0, i))
    out = pl.BlockSpec((rows, TILE), lambda i: (0, i))
    shape = jax.ShapeDtypeStruct((rows, width), jnp.bfloat16)
    return pl.pallas_call(
        project_body,
        grid=(width // TILE,),
        in_specs=[whole((count, depth))] * 4 + [whole((rows, HEAD_DIM))] * 2 + [column] * 3,
        out_specs=[out] * 3,
        out_shape=[shape] * 3,
        scratch_shapes=[pltpu.VMEM((rows, depth), jnp.bfloat16)],
        compiler_params=params(),
        cost_estimate=cost(False),
    )(*parts, cosine, sine, wq, wk, wv)


def attend_body(traded, q, k, v, *refs):
    own, came, refs = refs[:4], refs[4:8], refs[8:]
    of_row, of_column, wo, near, refs = refs[0], refs[1], refs[2], refs[3], refs[4:]
    far, (mixed, cached, weight, sems) = refs[:-4], refs[-4:]
    load = pltpu.make_async_copy(wo, weight, sems.at[4])
    count = own[0].shape[0]

    def fetch(blocks):
        copies = [
            pltpu.make_async_copy(block, cached.at[pl.ds(at * count, count), :], sems.at[at])
            for at, block in enumerate(blocks)
        ]
        for copy in copies:
            copy.start()
        load.start()
        for copy in copies:
            copy.wait()

    @pl.when(traded[0] == 1)
    def _():
        fetch(came)

    @pl.when(traded[0] != 1)
    def _():
        fetch(own)

    rows, width = q.shape
    heads = width // HEAD_DIM
    low, high = of_row[:, 0:1], of_row[:, 1:2]
    first, place = of_row[:, 2:3], of_row[:, 3:4]
    column = of_column[0:1, :]
    fresh = of_column[1:2, :rows]
    on_cached = (column >= low) & (column < high)
    on_fresh = (fresh >= first) & (fresh <= place)
    scale = 1.0 / math.sqrt(HEAD_DIM)
    contract_last = (((1,), (1,)), ((), ()))
    for head in range(heads):
        at = slice(head * HEAD_DIM, (head + 1) * HEAD_DIM)
        after = slice(width + head * HEAD_DIM, width + (head + 1) * HEAD_DIM)
        query = q[:, at]
        old = lax.dot_general(
            query, cached[:, at], contract_last, preferred_element_type=jnp.float32
        )
        new = lax.dot_general(query, k[:, at], contract_last, preferred_element_type=jnp.float32)
        old = jnp.where(on_cached, old * scale, MASKED)
        new = jnp.where(on_fresh, new * scale, MASKED)
        top = jnp.maximum(
            jnp.max(old, axis=-1, keepdims=True), jnp.max(new, axis=-1, keepdims=True)
        )
        old = jnp.exp(old - top)
        new = jnp.exp(new - top)
        share = 1.0 / (jnp.sum(old, axis=-1, keepdims=True) + jnp.sum(new, axis=-1, keepdims=True))
        sums = jnp.dot(
            (old * share).astype(jnp.bfloat16), cached[:, after], preferred_element_type=jnp.float32
        ) + jnp.dot(
            (new * share).astype(jnp.bfloat16), v[:, at], preferred_element_type=jnp.float32
        )
        mixed[:, at] = sums.astype(jnp.bfloat16)
    load.wait()
    left = mixed[...]
    for at in range(0, near.shape[1], TILE):
        part = jnp.dot(left, weight[:, at : at + TILE], preferred_element_type=jnp.float32)
        split_rows(part, at, near, far)


def split_rows(part, at, near, far):
    count, width = part.shape[0] // 4, far[0].shape[1]
    far, there = far[at // width], at % width
    near[:count, at : at + TILE] = part[:count]
    near[count:, at : at + TILE] = part[2 * count : 3 * count]
    far[:count, there : there + TILE] = part[count : 2 * count].astype(jnp.bfloat16)
    far[count:, there : there + TILE] = part[3 * count :].astype(jnp.bfloat16)


def split_shapes(rows, depth):
    return [jax.ShapeDtypeStruct((rows // 2, depth), jnp.float32)] + [
        jax.ShapeDtypeStruct((rows // 2, depth // FAR_PARTS), jnp.bfloat16)
    ] * FAR_PARTS


def attend(traded, q, k, v, own, came, of_row, of_column, wo):
    rows, width = q.shape
    depth = wo.shape[1]
    cached = of_column.shape[1]
    keys = cached + rows
    return pl.pallas_call(
        attend_body,
        in_specs=[smem()] + [vmem()] * 3 + [anywhere()] * 8 + [vmem()] * 2 + [anywhere()],
        out_specs=[vmem()] * (1 + FAR_PARTS),
        out_shape=split_shapes(rows, depth),
        scratch_shapes=[
            pltpu.VMEM((rows, width), jnp.bfloat16),
            pltpu.VMEM((cached, 2 * width), jnp.bfloat16),
            pltpu.VMEM(wo.shape, jnp.bfloat16),
            pltpu.SemaphoreType.DMA((5,)),
        ],
        compiler_params=params(),
        cost_estimate=cost(False),
    )(traded, q, k, v, *own, *came, of_row, of_column, wo)


def load_pieces(masks, info, wholes, pieces, held, sems):
    shard, width = wholes[0].shape[0], pieces[0].shape[1]
    columns = pl.ds(pl.multiple_of(info[MINE] * width, width), width)
    copies = []
    for at, mask in enumerate(masks):
        there = pl.ds(pl.multiple_of((info[WITHIN] ^ mask) * shard, shard), shard)
        for which, whole in enumerate(wholes):
            source = pieces[at - 1].at[pl.ds(which * shard, shard), :] if at else whole.at[:, columns]
            place = held.at[which, there, :]
            copies.append(pltpu.make_async_copy(source, place, sems.at[at, which]))
    for copy in copies:
        copy.start()
    return copies


def gate_up(masks, info, parts, gate, up, arrived):
    count, depth = parts[0].shape
    rows = len(parts) * count
    blocks, pieces = len(parts), len(arrived)
    width = arrived[0].shape[1]

    def body(info_ref, *refs):
        part_refs, refs = refs[:blocks], refs[blocks:]
        wholes, refs = refs[:2], refs[2:]
        piece_refs, refs = refs[:pieces], refs[pieces:]
        act_refs, (x, held, sems) = refs[:-3], refs[-3:]
        copies = load_pieces(masks, info_ref, wholes, piece_refs, held, sems)
        for at, block in enumerate(part_refs):
            x[pl.ds(at * count, count), :] = block[...]
        for copy in copies:
            copy.wait()
        for at in range(0, width, TILE):
            g = jnp.dot(x[...], held[0, :, at : at + TILE], preferred_element_type=jnp.float32)
            u = jnp.dot(x[...], held[1, :, at : at + TILE], preferred_element_type=jnp.float32)
            act = (g / (1.0 + jnp.exp(-g)) * u).astype(jnp.bfloat16)
            for group, act_ref in enumerate(act_refs):
                act_ref[:, at : at + TILE] = act[group * 4 * count : (group + 1) * 4 * count]

    return pl.pallas_call(
        body,
        in_specs=[smem()] + [vmem()] * blocks + [anywhere()] * (2 + pieces),
        out_specs=[vmem()] * (blocks // 4),
        out_shape=[jax.ShapeDtypeStruct((4 * count, width), jnp.bfloat16)] * (blocks // 4),
        scratch_shapes=[
            pltpu.VMEM((rows, depth), jnp.bfloat16),
            pltpu.VMEM((2, depth, width), jnp.bfloat16),
            pltpu.SemaphoreType.DMA((pieces + 1, 2)),
        ],
        compiler_params=params(),
        cost_estimate=cost(False),
    )(info, *parts, gate, up, *arrived)


def down_rows(masks, info, acts, down, arrived):
    rows, width = acts[0].shape
    groups, parts, pieces = len(acts), 1 + FAR_PARTS, len(arrived)
    depth = arrived[0].shape[0] * len(masks)

    def body(info_ref, *refs):
        act_refs, down_ref, refs = refs[:groups], refs[groups], refs[groups + 1 :]
        piece_refs, outs, (held, sems) = refs[:pieces], refs[pieces:-2], refs[-2:]
        for copy in load_pieces(masks, info_ref, [down_ref], piece_refs, held, sems):
            copy.wait()
        for group, act in enumerate(act_refs):
            near, *far = outs[group * parts : (group + 1) * parts]
            for at in range(0, depth, TILE):
                part = lax.dot_general(
                    act[...],
                    held[0, at : at + TILE, :],
                    (((1,), (1,)), ((), ())),
                    preferred_element_type=jnp.float32,
                )
                split_rows(part, at, near, far)

    sums = pl.pallas_call(
        body,
        in_specs=[smem()] + [vmem()] * groups + [anywhere()] * (1 + pieces),
        out_specs=[vmem()] * (groups * parts),
        out_shape=split_shapes(rows, depth) * groups,
        scratch_shapes=[
            pltpu.VMEM((1, depth, width), jnp.bfloat16),
            pltpu.SemaphoreType.DMA((pieces + 1, 1)),
        ],
        compiler_params=params(),
        cost_estimate=cost(False),
    )(info, *acts, down, *arrived)
    return [sums[at * parts : (at + 1) * parts] for at in range(groups)]


def gather_rows(rows, across=None):
    if across is None:
        across = swap(rows, "mp", 2)
    return [rows, swap(rows, "mp", 1), across, swap(across, "mp", 1)]


def over_core(parts):
    return [parts[0]] + [swap(part, "mp", 1) for part in parts[1:]]


def reduce_rows(near, *came, split=1):
    count = near.shape[0] // 2
    each = len(came) // split
    kept, sent = [], []
    for at in range(0, len(came), each):
        both = jnp.concatenate(came[at : at + each], axis=1).astype(jnp.float32)
        begin = at * came[0].shape[1]
        both = both + near[:, begin : begin + both.shape[1]]
        kept.append(both)
        sent.append(both[count:].astype(jnp.bfloat16))
    return kept, [swap(going, "mp", 2) for going in sent], sent


def over_cores(near, *far):
    came = jnp.concatenate([swap(part, "mp", 1) for part in far], axis=1)
    return near + came.astype(jnp.float32)


def total(kept, came):
    return [part[: more.shape[0]] + more.astype(jnp.float32) for part, more in zip(kept, came)]


def after(value, *earlier):
    return lax.optimization_barrier((value,) + earlier)[0] if earlier else value


def without(held, mask):
    return {at: piece for at, piece in held.items() if at != mask}


def join(*values):
    return lax.optimization_barrier(values)


def over_bits(held, bits):
    for bit in bits:
        held.update({mask ^ bit: swap(piece, "dp", bit) for mask, piece in list(held.items())})
    return held


def facts_body(info, lengths, requests, frequency, cosine, sine, of_row, of_column):
    rows = requests.shape[1]
    member, source = info[MEMBER], info[SOURCE]

    def places(size, axis, shape):
        at = lax.broadcasted_iota(jnp.int32, shape, axis)
        step = size // 4
        block = sum((at >= edge).astype(jnp.int32) for edge in (step, 2 * step, 3 * step))
        return at + ((member ^ block) - block) * step

    place = places(rows, 0, (rows, 1))
    request = requests[...]
    first, low = jnp.zeros_like(place), jnp.zeros_like(place)
    begin = lengths[source, 0]
    length = jnp.zeros_like(place) + begin
    for label in range(1, lengths.shape[1]):
        start = jnp.sum((request < label).astype(jnp.int32), axis=1, keepdims=True)
        reached = place >= start
        first = jnp.where(reached, start, first)
        low = jnp.where(reached, begin, low)
        length = jnp.where(reached, lengths[source, label], length)
        begin = begin + lengths[source, label]
    angle = (length + place - first).astype(jnp.float32) * frequency[...]
    cosine[...] = jnp.cos(angle)
    lane = lax.broadcasted_iota(jnp.int32, (1, HEAD_DIM), 1)
    sine[...] = jnp.sin(angle) * jnp.where(lane < HEAD_DIM // 2, -1.0, 1.0)
    column = lax.broadcasted_iota(jnp.int32, of_row.shape, 1)
    of_row[...] = jnp.where(
        column == 0, low, jnp.where(column == 1, low + length, jnp.where(column == 2, first, place))
    )
    of_column[0:1, :] = places(of_column.shape[1], 1, (1, of_column.shape[1]))
    of_column[1:2, :] = places(rows, 1, (1, of_column.shape[1]))


def row_facts(info, lengths, requests, cached):
    rows = requests.shape[1]
    half = HEAD_DIM // 2
    frequency = ROPE_BASE ** (-np.arange(half, dtype=np.float32) / np.float32(half))
    frequency = jnp.asarray(np.concatenate([frequency, frequency])[None], jnp.float32)
    turn = jax.ShapeDtypeStruct((rows, HEAD_DIM), jnp.float32)
    return pl.pallas_call(
        facts_body,
        in_specs=[smem(), smem(), vmem(), vmem()],
        out_specs=[vmem()] * 4,
        out_shape=[
            turn,
            turn,
            jax.ShapeDtypeStruct((rows, 8), jnp.int32),
            jax.ShapeDtypeStruct((8, cached), jnp.int32),
        ],
        compiler_params=params(),
        cost_estimate=cost(True),
    )(info, lengths, requests, frequency)


def finish_body(tokens, *refs):
    parts, (state, normed) = refs[:-2], refs[-2:]
    count = len(parts) // 2
    sums = jnp.concatenate(
        [
            parts[at][: tokens.shape[0], :] + parts[count + at][...].astype(jnp.float32)
            for at in range(count)
        ],
        axis=1,
    )
    rows = (tokens[...].astype(jnp.float32) + sums).astype(jnp.bfloat16)
    state[...] = rows
    normed[...] = layer_norm(rows.astype(jnp.float32)).astype(jnp.bfloat16)


def finish(tokens, kept, came):
    shape = jax.ShapeDtypeStruct(tokens.shape, jnp.bfloat16)
    return pl.pallas_call(
        finish_body,
        in_specs=[vmem()] * (1 + len(kept) + len(came)),
        out_specs=[vmem()] * 2,
        out_shape=[shape] * 2,
        compiler_params=params(),
        cost_estimate=cost(False),
    )(tokens, *kept, *came)


def local(
    tokens,
    request_ids,
    cache_entries,
    cached_lengths,
    traded,
    query_weight,
    key_weight,
    value_weight,
    output_weight,
    gate_weight,
    up_weight,
    down_weight,
):
    replica = lax.axis_index("rep")
    within = lax.axis_index("dp")
    member = lax.axis_index("mp")
    planes = lax.axis_size("dp")
    pair = planes // 2
    bits = [1 << at for at in range(planes.bit_length() - 1) if 1 << at != pair]
    place = (within // pair) % 2
    mine, leaving = 2 * place + replica, 2 * (1 - place) + replica
    source = jnp.where(traded[0] == 1, 1 - replica, replica) * planes + within
    info = jnp.stack([member, within, mine, leaving, source]).astype(jnp.int32)

    normed, *blocks, wide_leaving, wide_mine = prepare(
        info, tokens, cache_entries, gate_weight, up_weight
    )
    blocks = [blocks[0]] + [swap(blocks[mask], "mp", mask) for mask in (1, 2, 3)]
    facts = row_facts(info, cached_lengths, request_ids, 4 * cache_entries.shape[0])
    down_cut = cut(info, after(down_weight, wide_mine))
    came = [swap(block, "rep", 1) for block in blocks[:2]]
    came, blocks, facts, down_cut = join(came, blocks, facts, down_cut)
    came += [swap(block, "rep", 1) for block in blocks[2:]]
    parts = gather_rows(normed)

    def near_side(piece):
        return without(over_bits({0: piece}, bits), 0)

    def across(piece):
        return {pair: swap(piece, "dp", pair)}

    def far_side(held):
        return without(over_bits(dict(held), bits), pair)

    wide = {**across(wide_leaving), **near_side(wide_mine)}

    q, k, v = project(parts, facts[0], facts[1], query_weight, key_weight, value_weight)
    came, q = join(came, q)
    near, *far = attend(traded, q, k, v, blocks, came, facts[2], facts[3], output_weight)
    far = [swap(part, "mp", 1) for part in far]
    far, wide = join(far, wide)
    kept, came, _ = reduce_rows(near, *far, split=2)
    wide.update(far_side({pair: wide[pair]}))
    state_own, normed_own = finish(tokens, kept, came)

    rows_z = swap(normed_own, "dp", pair)
    rows_x = swap(normed_own, "rep", 1)
    over_chip = swap(rows_x, "mp", 2)
    rows_z, wide, over_chip = join(rows_z, wide, over_chip)
    parts = gather_rows(normed_own) + gather_rows(rows_x, over_chip)
    rows_both = swap(rows_z, "rep", 1)
    back = {**across(after(down_cut[0], rows_z)), **near_side(after(down_cut[1], rows_z))}
    parts += gather_rows(rows_z)
    masks = [0] + list(wide)
    in_order = lambda held: [held[mask] for mask in masks[1:]]
    acts = gate_up(masks, info, parts, gate_weight, up_weight, in_order(wide))
    acts, back = join(acts, back)
    back.update(far_side({pair: back[pair]}))
    parts = gather_rows(rows_both)
    parts[0] = after(parts[0], acts[0])
    acts += gate_up(masks, info, parts, gate_weight, up_weight, in_order(wide))

    def sums_of(*groups):
        return down_rows(masks, info, groups, down_weight, in_order(back))

    def crossed(value, axis, mask):
        return swap(value.astype(jnp.bfloat16), axis, mask).astype(jnp.float32)

    found_both, found_z = sums_of(acts[3], acts[2])
    kept, came, sent = reduce_rows(*over_core(found_both))
    kept_z, came_z, sent_z = reduce_rows(*over_core(found_z))
    found_x, found = sums_of(after(acts[1], *sent, *sent_z), acts[0])
    came, found_x, found = join(came, found_x, found)
    (of_both,), (of_z,) = total(kept, came), total(kept_z, came_z)
    sent = (of_z + crossed(of_both, "rep", 1)).astype(jnp.bfloat16)
    of_z = swap(sent, "dp", pair).astype(jnp.float32)
    (of_x,) = total(*reduce_rows(*over_core(found_x))[:2])
    (of_own,) = total(*reduce_rows(*over_core(found))[:2])
    of_x = after(of_x, sent)
    columns = of_x.shape[1]
    of_x = [crossed(of_x[:, at : at + columns // 2], "rep", 1) for at in (0, columns // 2)]
    of_own = of_own + jnp.concatenate(of_x, axis=1)
    return (state_own.astype(jnp.float32) + (of_own + of_z)).astype(jnp.bfloat16)


def solution(mesh):
    in_specs = (
        P(("rep", "dp", "mp"), None),
        P(("rep", "dp"), None),
        P(("rep", "dp", "mp"), None),
        P(),
        P("dp"),
        P(None, "mp"),
        P(None, "mp"),
        P(None, "mp"),
        P("mp", None),
        P("dp", "mp"),
        P("dp", "mp"),
        P("dp", "mp"),
    )
    out_specs = P(("rep", "dp", "mp"), None)
    return jax.shard_map(local, mesh=mesh, in_specs=in_specs, out_specs=out_specs, check_vma=False)
```

```python
import math

import jax
import jax.numpy as jnp
import numpy as np
from jax import lax
from jax.experimental import pallas as pl
from jax.experimental.pallas import tpu as pltpu
from jax.sharding import PartitionSpec as P

HEAD_DIM = 128
EPSILON = 1e-05
ROPE_BASE = 10000.0
VMEM_LIMIT = 60 * 1024 * 1024
TILE = 256
MASKED = -1e30
MEMBER, WITHIN, MINE, LEAVING, SOURCE = range(5)


def swap(value, axis, mask):
    pairs = [(source, source ^ mask) for source in range(lax.axis_size(axis))]
    return lax.ppermute(value, axis, pairs)


def layer_norm(rows):
    center = rows - jnp.mean(rows, axis=-1, keepdims=True)
    spread = jnp.mean(center * center, axis=-1, keepdims=True)
    return center * lax.rsqrt(spread + EPSILON)


def vmem():
    return pl.BlockSpec(memory_space=pltpu.VMEM)


def smem():
    return pl.BlockSpec(memory_space=pltpu.SMEM)


def anywhere():
    return pl.BlockSpec(memory_space=pl.ANY)


def params():
    return pltpu.CompilerParams(vmem_limit_bytes=VMEM_LIMIT)


def cost(gate=True):
    return pl.CostEstimate(flops=10**11 if gate else 0, bytes_accessed=0, transcendentals=0)


def prepare(info, tokens, entries, *weights):
    rows, columns = entries.shape
    stack, depth, width = len(weights), weights[0].shape[0], weights[0].shape[1] // 4

    def body(info_ref, token_ref, entry_ref, *refs):
        sources, normed, blocks = refs[:stack], refs[stack], refs[stack + 1 : stack + 5]
        outs, sems = refs[stack + 5 : -1], refs[-1]
        copies = cut_copies(info_ref, sources, outs, sems)
        part = blocks[0].shape[1] // 2
        for mask, out in enumerate(blocks):
            begin = pl.multiple_of((info_ref[MEMBER] ^ mask) * part, part)
            out[:, :part] = entry_ref[:, pl.ds(begin, part)]
            out[:, part:] = entry_ref[:, pl.ds(4 * part + begin, part)]
        normed[...] = layer_norm(token_ref[...].astype(jnp.float32)).astype(jnp.bfloat16)
        for copy in copies:
            copy.wait()

    return pl.pallas_call(
        body,
        in_specs=[smem(), vmem(), vmem()] + [anywhere()] * stack,
        out_specs=[vmem()] * 7,
        out_shape=[jax.ShapeDtypeStruct(tokens.shape, jnp.bfloat16)]
        + [jax.ShapeDtypeStruct((rows, columns // 4), jnp.bfloat16)] * 4
        + [jax.ShapeDtypeStruct((stack * depth, width), jnp.bfloat16)] * 2,
        scratch_shapes=[pltpu.SemaphoreType.DMA((2, stack))],
        compiler_params=params(),
        cost_estimate=cost(False),
    )(info, tokens, entries, *weights)


def cut_copies(info, sources, outs, sems):
    rows = sources[0].shape[0]
    width = outs[0].shape[1]
    copies = []
    for at, out in enumerate(outs):
        there = pl.ds(pl.multiple_of(info[(LEAVING, MINE)[at]] * width, width), width)
        for which, source in enumerate(sources):
            place = out.at[pl.ds(which * rows, rows), :]
            copies.append(pltpu.make_async_copy(source.at[:, there], place, sems.at[at, which]))
    for copy in copies:
        copy.start()
    return copies


def cut(info, *weights):
    rows, columns = weights[0].shape
    width = columns // 4
    count, stack = 2, len(weights)

    def body(info_ref, *refs):
        for copy in cut_copies(info_ref, refs[:stack], refs[stack:-1], refs[-1]):
            copy.wait()

    return pl.pallas_call(
        body,
        in_specs=[smem()] + [anywhere()] * stack,
        out_specs=[vmem()] * count,
        out_shape=[jax.ShapeDtypeStruct((stack * rows, width), jnp.bfloat16)] * count,
        scratch_shapes=[pltpu.SemaphoreType.DMA((count, stack))],
        compiler_params=params(),
        cost_estimate=cost(False),
    )(info, *weights)


def project_body(n0, n1, n2, n3, cosine, sine, wq, wk, wv, q_ref, k_ref, v_ref, rows):
    count = n0.shape[0]

    @pl.when(pl.program_id(0) == 0)
    def _():
        for at, part in enumerate((n0, n1, n2, n3)):
            rows[pl.ds(at * count, count), :] = part[...]

    x = rows[...]
    width = wq.shape[1]
    for weight, out, turned in ((wq, q_ref, True), (wk, k_ref, True), (wv, v_ref, False)):
        product = jnp.dot(x, weight[...], preferred_element_type=jnp.float32)
        if not turned:
            out[...] = product.astype(jnp.bfloat16)
            continue
        for at in range(0, width, HEAD_DIM):
            head = product[:, at : at + HEAD_DIM]
            other = pltpu.roll(head, HEAD_DIM // 2, 1)
            out[:, at : at + HEAD_DIM] = (head * cosine[...] + other * sine[...]).astype(
                jnp.bfloat16
            )


def project(parts, cosine, sine, wq, wk, wv):
    count, depth = parts[0].shape
    rows, width = 4 * count, wq.shape[1]
    whole = lambda shape: pl.BlockSpec(shape, lambda i: (0, 0))
    column = pl.BlockSpec((depth, TILE), lambda i: (0, i))
    out = pl.BlockSpec((rows, TILE), lambda i: (0, i))
    shape = jax.ShapeDtypeStruct((rows, width), jnp.bfloat16)
    return pl.pallas_call(
        project_body,
        grid=(width // TILE,),
        in_specs=[whole((count, depth))] * 4 + [whole((rows, HEAD_DIM))] * 2 + [column] * 3,
        out_specs=[out] * 3,
        out_shape=[shape] * 3,
        scratch_shapes=[pltpu.VMEM((rows, depth), jnp.bfloat16)],
        compiler_params=params(),
        cost_estimate=cost(False),
    )(*parts, cosine, sine, wq, wk, wv)


def attend_body(traded, q, k, v, *refs):
    own, came, refs = refs[:4], refs[4:8], refs[8:]
    of_row, of_column, wo, refs = refs[0], refs[1], refs[2], refs[3:]
    outs, (mixed, cached, weight, sems) = refs[:-4], refs[-4:]
    load = pltpu.make_async_copy(wo, weight, sems.at[4])
    count = own[0].shape[0]

    def fetch(blocks):
        copies = [
            pltpu.make_async_copy(block, cached.at[pl.ds(at * count, count), :], sems.at[at])
            for at, block in enumerate(blocks)
        ]
        for copy in copies:
            copy.start()
        load.start()
        for copy in copies:
            copy.wait()

    @pl.when(traded[0] == 1)
    def _():
        fetch(came)

    @pl.when(traded[0] != 1)
    def _():
        fetch(own)

    rows, width = q.shape
    heads = width // HEAD_DIM
    low, high = of_row[:, 0:1], of_row[:, 1:2]
    first, place = of_row[:, 2:3], of_row[:, 3:4]
    column = of_column[0:1, :]
    fresh = of_column[1:2, :rows]
    on_cached = (column >= low) & (column < high)
    on_fresh = (fresh >= first) & (fresh <= place)
    scale = 1.0 / math.sqrt(HEAD_DIM)
    contract_last = (((1,), (1,)), ((), ()))
    for head in range(heads):
        at = slice(head * HEAD_DIM, (head + 1) * HEAD_DIM)
        after = slice(width + head * HEAD_DIM, width + (head + 1) * HEAD_DIM)
        query = q[:, at]
        old = lax.dot_general(
            query, cached[:, at], contract_last, preferred_element_type=jnp.float32
        )
        new = lax.dot_general(query, k[:, at], contract_last, preferred_element_type=jnp.float32)
        old = jnp.where(on_cached, old * scale, MASKED)
        new = jnp.where(on_fresh, new * scale, MASKED)
        top = jnp.maximum(
            jnp.max(old, axis=-1, keepdims=True), jnp.max(new, axis=-1, keepdims=True)
        )
        old = jnp.exp(old - top)
        new = jnp.exp(new - top)
        share = 1.0 / (jnp.sum(old, axis=-1, keepdims=True) + jnp.sum(new, axis=-1, keepdims=True))
        sums = jnp.dot(
            (old * share).astype(jnp.bfloat16), cached[:, after], preferred_element_type=jnp.float32
        ) + jnp.dot(
            (new * share).astype(jnp.bfloat16), v[:, at], preferred_element_type=jnp.float32
        )
        mixed[:, at] = sums.astype(jnp.bfloat16)
    load.wait()
    left = mixed[...]
    for at in range(0, weight.shape[1], TILE):
        part = jnp.dot(left, weight[:, at : at + TILE], preferred_element_type=jnp.float32)
        split_rows(part, at, outs)


def split_rows(part, at, outs):
    count = part.shape[0] // 4
    for out, block in zip(outs, (0, 2, 1, 3)):
        rows = part[block * count : (block + 1) * count]
        out[:, at : at + TILE] = rows.astype(out.dtype)


def split_shapes(rows, depth):
    return [
        jax.ShapeDtypeStruct((rows // 4, depth), kind)
        for kind in (jnp.float32, jnp.float32, jnp.bfloat16, jnp.bfloat16)
    ]


def attend(traded, q, k, v, own, came, of_row, of_column, wo):
    rows, width = q.shape
    depth = wo.shape[1]
    cached = of_column.shape[1]
    keys = cached + rows
    return pl.pallas_call(
        attend_body,
        in_specs=[smem()] + [vmem()] * 3 + [anywhere()] * 8 + [vmem()] * 2 + [anywhere()],
        out_specs=[vmem()] * 4,
        out_shape=split_shapes(rows, depth),
        scratch_shapes=[
            pltpu.VMEM((rows, width), jnp.bfloat16),
            pltpu.VMEM((cached, 2 * width), jnp.bfloat16),
            pltpu.VMEM(wo.shape, jnp.bfloat16),
            pltpu.SemaphoreType.DMA((5,)),
        ],
        compiler_params=params(),
        cost_estimate=cost(False),
    )(traded, q, k, v, *own, *came, of_row, of_column, wo)


def load_pieces(masks, info, wholes, pieces, held, sems):
    shard, width = wholes[0].shape[0], pieces[0].shape[1]
    columns = pl.ds(pl.multiple_of(info[MINE] * width, width), width)
    copies = []
    for at, mask in enumerate(masks):
        there = pl.ds(pl.multiple_of((info[WITHIN] ^ mask) * shard, shard), shard)
        for which, whole in enumerate(wholes):
            source = pieces[at - 1].at[pl.ds(which * shard, shard), :] if at else whole.at[:, columns]
            place = held.at[which, there, :]
            copies.append(pltpu.make_async_copy(source, place, sems.at[at, which]))
    for copy in copies:
        copy.start()
    return copies


def gate_up(masks, info, parts, gate, up, arrived):
    count, depth = parts[0].shape
    rows = len(parts) * count
    blocks, pieces = len(parts), len(arrived)
    width = arrived[0].shape[1]

    def body(info_ref, *refs):
        part_refs, refs = refs[:blocks], refs[blocks:]
        wholes, refs = refs[:2], refs[2:]
        piece_refs, refs = refs[:pieces], refs[pieces:]
        act_refs, (x, held, sems) = refs[:-3], refs[-3:]
        copies = load_pieces(masks, info_ref, wholes, piece_refs, held, sems)
        for at, block in enumerate(part_refs):
            x[pl.ds(at * count, count), :] = block[...]
        for copy in copies:
            copy.wait()
        for at in range(0, width, TILE):
            g = jnp.dot(x[...], held[0, :, at : at + TILE], preferred_element_type=jnp.float32)
            u = jnp.dot(x[...], held[1, :, at : at + TILE], preferred_element_type=jnp.float32)
            act = (g / (1.0 + jnp.exp(-g)) * u).astype(jnp.bfloat16)
            for group, act_ref in enumerate(act_refs):
                act_ref[:, at : at + TILE] = act[group * 4 * count : (group + 1) * 4 * count]

    return pl.pallas_call(
        body,
        in_specs=[smem()] + [vmem()] * blocks + [anywhere()] * (2 + pieces),
        out_specs=[vmem()] * (blocks // 4),
        out_shape=[jax.ShapeDtypeStruct((4 * count, width), jnp.bfloat16)] * (blocks // 4),
        scratch_shapes=[
            pltpu.VMEM((rows, depth), jnp.bfloat16),
            pltpu.VMEM((2, depth, width), jnp.bfloat16),
            pltpu.SemaphoreType.DMA((pieces + 1, 2)),
        ],
        compiler_params=params(),
        cost_estimate=cost(False),
    )(info, *parts, gate, up, *arrived)


def down_rows(masks, info, acts, down, arrived, gate=False):
    rows, width = acts[0].shape
    groups, pieces = len(acts), len(arrived)
    depth = arrived[0].shape[0] * len(masks)

    def body(info_ref, *refs):
        act_refs, down_ref, refs = refs[:groups], refs[groups], refs[groups + 1 :]
        piece_refs, outs, (held, sems) = refs[:pieces], refs[pieces:-2], refs[-2:]
        for copy in load_pieces(masks, info_ref, [down_ref], piece_refs, held, sems):
            copy.wait()
        for group, act in enumerate(act_refs):
            for at in range(0, depth, TILE):
                part = lax.dot_general(
                    act[...],
                    held[0, at : at + TILE, :],
                    (((1,), (1,)), ((), ())),
                    preferred_element_type=jnp.float32,
                )
                split_rows(part, at, outs[4 * group : 4 * group + 4])

    sums = pl.pallas_call(
        body,
        in_specs=[smem()] + [vmem()] * groups + [anywhere()] * (1 + pieces),
        out_specs=[vmem()] * (4 * groups),
        out_shape=split_shapes(rows, depth) * groups,
        scratch_shapes=[
            pltpu.VMEM((1, depth, width), jnp.bfloat16),
            pltpu.SemaphoreType.DMA((pieces + 1, 1)),
        ],
        compiler_params=params(),
        cost_estimate=cost(gate),
    )(info, *acts, down, *arrived)
    return [sums[4 * at : 4 * at + 4] for at in range(groups)]


def gather_rows(rows, across=None):
    if across is None:
        across = swap(rows, "mp", 2)
    return [rows, swap(rows, "mp", 1), across, swap(across, "mp", 1)]


def reduce_rows(own, across, far_own, far_across):
    sent = (across + swap(far_across, "mp", 1).astype(jnp.float32)).astype(jnp.bfloat16)
    return (own, swap(far_own, "mp", 1)), swap(sent, "mp", 2), sent


def total(kept, came):
    own, other = kept
    return own + other.astype(jnp.float32) + came.astype(jnp.float32)


def after(value, *earlier):
    return lax.optimization_barrier((value,) + earlier)[0] if earlier else value


def without(held, mask):
    return {at: piece for at, piece in held.items() if at != mask}


def join(*values):
    return lax.optimization_barrier(values)


def over_bits(held, bits):
    for bit in bits:
        held.update({mask ^ bit: swap(piece, "dp", bit) for mask, piece in list(held.items())})
    return held


def facts_body(info, lengths, requests, frequency, cosine, sine, of_row, of_column):
    rows = requests.shape[1]
    member, source = info[MEMBER], info[SOURCE]

    def places(size, axis, shape):
        at = lax.broadcasted_iota(jnp.int32, shape, axis)
        step = size // 4
        block = sum((at >= edge).astype(jnp.int32) for edge in (step, 2 * step, 3 * step))
        return at + ((member ^ block) - block) * step

    place = places(rows, 0, (rows, 1))
    request = requests[...]
    first, low = jnp.zeros_like(place), jnp.zeros_like(place)
    begin = lengths[source, 0]
    length = jnp.zeros_like(place) + begin
    for label in range(1, lengths.shape[1]):
        start = jnp.sum((request < label).astype(jnp.int32), axis=1, keepdims=True)
        reached = place >= start
        first = jnp.where(reached, start, first)
        low = jnp.where(reached, begin, low)
        length = jnp.where(reached, lengths[source, label], length)
        begin = begin + lengths[source, label]
    angle = (length + place - first).astype(jnp.float32) * frequency[...]
    cosine[...] = jnp.cos(angle)
    lane = lax.broadcasted_iota(jnp.int32, (1, HEAD_DIM), 1)
    sine[...] = jnp.sin(angle) * jnp.where(lane < HEAD_DIM // 2, -1.0, 1.0)
    column = lax.broadcasted_iota(jnp.int32, of_row.shape, 1)
    of_row[...] = jnp.where(
        column == 0, low, jnp.where(column == 1, low + length, jnp.where(column == 2, first, place))
    )
    of_column[0:1, :] = places(of_column.shape[1], 1, (1, of_column.shape[1]))
    of_column[1:2, :] = places(rows, 1, (1, of_column.shape[1]))


def row_facts(info, lengths, requests, cached):
    rows = requests.shape[1]
    half = HEAD_DIM // 2
    frequency = ROPE_BASE ** (-np.arange(half, dtype=np.float32) / np.float32(half))
    frequency = jnp.asarray(np.concatenate([frequency, frequency])[None], jnp.float32)
    turn = jax.ShapeDtypeStruct((rows, HEAD_DIM), jnp.float32)
    return pl.pallas_call(
        facts_body,
        in_specs=[smem(), smem(), vmem(), vmem()],
        out_specs=[vmem()] * 4,
        out_shape=[
            turn,
            turn,
            jax.ShapeDtypeStruct((rows, 8), jnp.int32),
            jax.ShapeDtypeStruct((8, cached), jnp.int32),
        ],
        compiler_params=params(),
        cost_estimate=cost(False),
    )(info, lengths, requests, frequency)


def local(
    tokens,
    request_ids,
    cache_entries,
    cached_lengths,
    traded,
    query_weight,
    key_weight,
    value_weight,
    output_weight,
    gate_weight,
    up_weight,
    down_weight,
):
    replica = lax.axis_index("rep")
    within = lax.axis_index("dp")
    member = lax.axis_index("mp")
    planes = lax.axis_size("dp")
    pair = planes // 2
    bits = [1 << at for at in range(planes.bit_length() - 1) if 1 << at != pair]
    place = (within // pair) % 2
    mine, leaving = 2 * place + replica, 2 * (1 - place) + replica
    source = jnp.where(traded[0] == 1, 1 - replica, replica) * planes + within
    info = jnp.stack([member, within, mine, leaving, source]).astype(jnp.int32)

    normed, *blocks, wide_leaving, wide_mine = prepare(
        info, tokens, cache_entries, gate_weight, up_weight
    )
    blocks = [blocks[0]] + [swap(blocks[mask], "mp", mask) for mask in (1, 2, 3)]
    facts = row_facts(info, cached_lengths, request_ids, 4 * cache_entries.shape[0])
    came = [swap(block, "rep", 1) for block in blocks]
    over_chip = swap(normed, "mp", 2)
    over_chip, came[0], came[1] = join(over_chip, came[0], came[1])
    parts = gather_rows(normed, over_chip)

    def near_side(piece):
        return without(over_bits({0: piece}, bits), 0)

    def across(piece):
        return {pair: swap(piece, "dp", pair)}

    def far_side(held):
        return without(over_bits(dict(held), bits), pair)

    wide = {**across(wide_leaving), **near_side(after(wide_mine, blocks[1]))}

    q, k, v = project(parts, facts[0], facts[1], query_weight, key_weight, value_weight)
    came, q = join(came, q)
    sums = attend(traded, q, k, v, blocks, came, facts[2], facts[3], output_weight)
    sums, wide = join(sums, wide)
    kept, came, sent = reduce_rows(*sums)
    down_cut = cut(info, after(down_weight, sent))
    kept, came, down_cut = join(kept, came, down_cut)
    wide.update(far_side({pair: wide[pair]}))
    state_own = (tokens.astype(jnp.float32) + total(kept, came)).astype(jnp.bfloat16)
    normed_own = layer_norm(state_own.astype(jnp.float32)).astype(jnp.bfloat16)

    rows_z = swap(normed_own, "dp", pair)
    rows_x = swap(normed_own, "rep", 1)
    over_chip = swap(normed_own, "mp", 2), swap(rows_x, "mp", 2)
    rows_z, wide, over_chip = join(rows_z, wide, over_chip)
    parts = gather_rows(normed_own, over_chip[0]) + gather_rows(rows_x, over_chip[1])
    rows_both = swap(rows_z, "rep", 1)
    back = {**across(after(down_cut[0], rows_z)), **near_side(after(down_cut[1], rows_z))}
    parts += gather_rows(rows_z)
    masks = [0] + list(wide)
    in_order = lambda held: [held[mask] for mask in masks[1:]]
    acts = gate_up(masks, info, parts, gate_weight, up_weight, in_order(wide))
    parts = gather_rows(rows_both)
    parts[0] = after(parts[0], acts[0])
    acts, back = join(acts, back)
    back.update(far_side({pair: back[pair]}))
    acts += gate_up(masks, info, parts, gate_weight, up_weight, in_order(wide))

    def sums_of(*groups, gate=False):
        return down_rows(masks, info, groups, down_weight, in_order(back), gate)

    def crossed(value, axis, mask):
        return swap(value.astype(jnp.bfloat16), axis, mask).astype(jnp.float32)

    found_both, found_z = sums_of(acts[3], acts[2])
    kept, came, sent = reduce_rows(*found_both)
    kept_z, came_z, sent_z = reduce_rows(*found_z)
    found_x, found = sums_of(after(acts[1], sent, sent_z), acts[0], gate=True)
    came, found_x, found = join(came, found_x, found)
    of_both, of_z = total(kept, came), total(kept_z, came_z)
    of_both = of_both.astype(jnp.bfloat16)
    sent = (of_z + crossed(of_both, "rep", 1)).astype(jnp.bfloat16)
    of_z = swap(sent, "dp", pair).astype(jnp.float32)
    found_x, found = after((found_x, found), of_both)
    kept, came, sent_x = reduce_rows(*found_x)
    of_x = total(kept, came)
    of_own = total(*reduce_rows(*after(found, sent_x))[:2])
    of_x = after(of_x, sent)
    columns = of_x.shape[1]
    of_x = [crossed(of_x[:, at : at + columns // 2], "rep", 1) for at in (0, columns // 2)]
    of_own = of_own + jnp.concatenate(of_x, axis=1)
    return (state_own.astype(jnp.float32) + (of_own + of_z)).astype(jnp.bfloat16)


def solution(mesh):
    in_specs = (
        P(("rep", "dp", "mp"), None),
        P(("rep", "dp"), None),
        P(("rep", "dp", "mp"), None),
        P(),
        P("dp"),
        P(None, "mp"),
        P(None, "mp"),
        P(None, "mp"),
        P("mp", None),
        P("dp", "mp"),
        P("dp", "mp"),
        P("dp", "mp"),
    )
    out_specs = P(("rep", "dp", "mp"), None)
    return jax.shard_map(local, mesh=mesh, in_specs=in_specs, out_specs=out_specs, check_vma=False)
```

```python
import math

import jax
import jax.numpy as jnp
import numpy as np
from jax import lax
from jax.experimental import pallas as pl
from jax.experimental.pallas import tpu as pltpu
from jax.sharding import PartitionSpec as P

HEAD_DIM = 128
EPSILON = 1e-05
ROPE_BASE = 10000.0
VMEM_LIMIT = 28 * 1024 * 1024
VMEM_WHOLE = 60 * 1024 * 1024
TILE = 256
MASKED = -1e30
MEMBER, WITHIN, MINE, LEAVING, SOURCE = range(5)


def swap(value, axis, mask):
    pairs = [(source, source ^ mask) for source in range(lax.axis_size(axis))]
    return lax.ppermute(value, axis, pairs)


def layer_norm(rows):
    center = rows - jnp.mean(rows, axis=-1, keepdims=True)
    spread = jnp.mean(center * center, axis=-1, keepdims=True)
    return center * lax.rsqrt(spread + EPSILON)


def vmem():
    return pl.BlockSpec(memory_space=pltpu.VMEM)


def smem():
    return pl.BlockSpec(memory_space=pltpu.SMEM)


def anywhere():
    return pl.BlockSpec(memory_space=pl.ANY)


def params(limit=VMEM_LIMIT):
    return pltpu.CompilerParams(vmem_limit_bytes=limit)


def cost(gate=True):
    return pl.CostEstimate(flops=10**11 if gate else 0, bytes_accessed=0, transcendentals=0)


def prepare(info, tokens, entries, *weights):
    rows, columns = entries.shape
    stack, depth, width = len(weights), weights[0].shape[0], weights[0].shape[1] // 4

    def body(info_ref, token_ref, entry_ref, *refs):
        sources, normed, blocks = refs[:stack], refs[stack : stack + 2], refs[stack + 2 : stack + 6]
        outs, sems = refs[stack + 6 : -1], refs[-1]
        copies = cut_copies(info_ref, sources, outs, sems)
        part = blocks[0].shape[1] // 2
        for mask, out in enumerate(blocks):
            begin = pl.multiple_of((info_ref[MEMBER] ^ mask) * part, part)
            out[:, :part] = entry_ref[:, pl.ds(begin, part)]
            out[:, part:] = entry_ref[:, pl.ds(4 * part + begin, part)]
        found = layer_norm(token_ref[...].astype(jnp.float32)).astype(jnp.bfloat16)
        for half, out in enumerate(normed):
            out[...] = found[:, half * out.shape[1] : (half + 1) * out.shape[1]]
        for copy in copies:
            copy.wait()

    return pl.pallas_call(
        body,
        in_specs=[smem(), vmem(), vmem()] + [anywhere()] * stack,
        out_specs=[vmem()] * 8,
        out_shape=[jax.ShapeDtypeStruct((tokens.shape[0], tokens.shape[1] // 2), jnp.bfloat16)] * 2
        + [jax.ShapeDtypeStruct((rows, columns // 4), jnp.bfloat16)] * 4
        + [jax.ShapeDtypeStruct((stack * depth, width), jnp.bfloat16)] * 2,
        scratch_shapes=[pltpu.SemaphoreType.DMA((2, stack))],
        compiler_params=params(VMEM_WHOLE),
        cost_estimate=cost(False),
    )(info, tokens, entries, *weights)


def cut_copies(info, sources, outs, sems):
    rows = sources[0].shape[0]
    width = outs[0].shape[1]
    copies = []
    for at, out in enumerate(outs):
        there = pl.ds(pl.multiple_of(info[(LEAVING, MINE)[at]] * width, width), width)
        for which, source in enumerate(sources):
            place = out.at[pl.ds(which * rows, rows), :]
            copies.append(pltpu.make_async_copy(source.at[:, there], place, sems.at[at, which]))
    for copy in copies:
        copy.start()
    return copies


def cut(info, *weights):
    rows, columns = weights[0].shape
    width = columns // 4
    count, stack = 2, len(weights)

    def body(info_ref, *refs):
        for copy in cut_copies(info_ref, refs[:stack], refs[stack:-1], refs[-1]):
            copy.wait()

    return pl.pallas_call(
        body,
        in_specs=[smem()] + [anywhere()] * stack,
        out_specs=[vmem()] * count,
        out_shape=[jax.ShapeDtypeStruct((stack * rows, width), jnp.bfloat16)] * count,
        scratch_shapes=[pltpu.SemaphoreType.DMA((count, stack))],
        compiler_params=params(),
        cost_estimate=cost(False),
    )(info, *weights)


def project_body(*refs):
    parts, refs = refs[:8], refs[8:]
    cosine, sine, wq, wk, wv, q_ref, k_ref, v_ref, rows = refs
    count, half = parts[0].shape

    @pl.when(pl.program_id(0) == 0)
    def _():
        for at, part in enumerate(parts):
            begin = at % 2 * half
            rows[pl.ds(at // 2 * count, count), begin : begin + half] = part[...]

    x = rows[...]
    width = wq.shape[1]
    for weight, out, turned in ((wq, q_ref, True), (wk, k_ref, True), (wv, v_ref, False)):
        product = jnp.dot(x, weight[...], preferred_element_type=jnp.float32)
        if not turned:
            out[...] = product.astype(jnp.bfloat16)
            continue
        for at in range(0, width, HEAD_DIM):
            head = product[:, at : at + HEAD_DIM]
            other = pltpu.roll(head, HEAD_DIM // 2, 1)
            out[:, at : at + HEAD_DIM] = (head * cosine[...] + other * sine[...]).astype(
                jnp.bfloat16
            )


def project(parts, cosine, sine, wq, wk, wv):
    count, depth = parts[0].shape[0], 2 * parts[0].shape[1]
    rows, width = 4 * count, wq.shape[1]
    whole = lambda shape: pl.BlockSpec(shape, lambda i: (0, 0))
    column = pl.BlockSpec((depth, TILE), lambda i: (0, i))
    out = pl.BlockSpec((rows, TILE), lambda i: (0, i))
    shape = jax.ShapeDtypeStruct((rows, width), jnp.bfloat16)
    return pl.pallas_call(
        project_body,
        grid=(width // TILE,),
        in_specs=[whole((count, depth // 2))] * 8 + [whole((rows, HEAD_DIM))] * 2 + [column] * 3,
        out_specs=[out] * 3,
        out_shape=[shape] * 3,
        scratch_shapes=[pltpu.VMEM((rows, depth), jnp.bfloat16)],
        compiler_params=params(),
        cost_estimate=cost(False),
    )(*parts, cosine, sine, wq, wk, wv)


def attend_body(traded, q, k, v, *refs):
    own, came, refs = refs[:4], refs[4:8], refs[8:]
    of_row, of_column, wo, refs = refs[0], refs[1], refs[2], refs[3:]
    outs, (mixed, cached, weight, sems) = refs[:-4], refs[-4:]
    load = pltpu.make_async_copy(wo, weight, sems.at[4])
    count = own[0].shape[0]

    def fetch(blocks):
        copies = [
            pltpu.make_async_copy(block, cached.at[pl.ds(at * count, count), :], sems.at[at])
            for at, block in enumerate(blocks)
        ]
        for copy in copies:
            copy.start()
        load.start()
        for copy in copies:
            copy.wait()

    @pl.when(traded[0] == 1)
    def _():
        fetch(came)

    @pl.when(traded[0] != 1)
    def _():
        fetch(own)

    rows, width = q.shape
    heads = width // HEAD_DIM
    low, high = of_row[:, 0:1], of_row[:, 1:2]
    first, place = of_row[:, 2:3], of_row[:, 3:4]
    column = of_column[0:1, :]
    fresh = of_column[1:2, :rows]
    on_cached = (column >= low) & (column < high)
    on_fresh = (fresh >= first) & (fresh <= place)
    scale = 1.0 / math.sqrt(HEAD_DIM)
    contract_last = (((1,), (1,)), ((), ()))
    for head in range(heads):
        at = slice(head * HEAD_DIM, (head + 1) * HEAD_DIM)
        after = slice(width + head * HEAD_DIM, width + (head + 1) * HEAD_DIM)
        query = q[:, at]
        old = lax.dot_general(
            query, cached[:, at], contract_last, preferred_element_type=jnp.float32
        )
        new = lax.dot_general(query, k[:, at], contract_last, preferred_element_type=jnp.float32)
        old = jnp.where(on_cached, old * scale, MASKED)
        new = jnp.where(on_fresh, new * scale, MASKED)
        top = jnp.maximum(
            jnp.max(old, axis=-1, keepdims=True), jnp.max(new, axis=-1, keepdims=True)
        )
        old = jnp.exp(old - top)
        new = jnp.exp(new - top)
        share = 1.0 / (jnp.sum(old, axis=-1, keepdims=True) + jnp.sum(new, axis=-1, keepdims=True))
        sums = jnp.dot(
            (old * share).astype(jnp.bfloat16), cached[:, after], preferred_element_type=jnp.float32
        ) + jnp.dot(
            (new * share).astype(jnp.bfloat16), v[:, at], preferred_element_type=jnp.float32
        )
        mixed[:, at] = sums.astype(jnp.bfloat16)
    load.wait()
    left = mixed[...]
    for at in range(0, weight.shape[1], TILE):
        part = jnp.dot(left, weight[:, at : at + TILE], preferred_element_type=jnp.float32)
        split_rows(part, at, outs)


def split_rows(part, at, outs):
    count = part.shape[0] // 4
    for out, block in zip(outs, (0, 2, 1, 3)):
        rows = part[block * count : (block + 1) * count]
        out[:, at : at + TILE] = rows.astype(out.dtype)


def split_shapes(rows, depth):
    return [
        jax.ShapeDtypeStruct((rows // 4, depth), kind)
        for kind in (jnp.float32, jnp.float32, jnp.bfloat16, jnp.bfloat16)
    ]


def attend(traded, q, k, v, own, came, of_row, of_column, wo):
    rows, width = q.shape
    depth = wo.shape[1]
    cached = of_column.shape[1]
    keys = cached + rows
    return pl.pallas_call(
        attend_body,
        in_specs=[smem()] + [vmem()] * 3 + [anywhere()] * 8 + [vmem()] * 2 + [anywhere()],
        out_specs=[vmem()] * 4,
        out_shape=split_shapes(rows, depth),
        scratch_shapes=[
            pltpu.VMEM((rows, width), jnp.bfloat16),
            pltpu.VMEM((cached, 2 * width), jnp.bfloat16),
            pltpu.VMEM(wo.shape, jnp.bfloat16),
            pltpu.SemaphoreType.DMA((5,)),
        ],
        compiler_params=params(),
        cost_estimate=cost(False),
    )(traded, q, k, v, *own, *came, of_row, of_column, wo)


def load_pieces(masks, info, wholes, pieces, held, sems):
    shard, width = wholes[0].shape[0], pieces[0].shape[1]
    columns = pl.ds(pl.multiple_of(info[MINE] * width, width), width)
    copies = []
    for at, mask in enumerate(masks):
        there = pl.ds(pl.multiple_of((info[WITHIN] ^ mask) * shard, shard), shard)
        for which, whole in enumerate(wholes):
            source = pieces[at - 1].at[pl.ds(which * shard, shard), :] if at else whole.at[:, columns]
            place = held.at[which, there, :]
            copies.append(pltpu.make_async_copy(source, place, sems.at[at, which]))
    for copy in copies:
        copy.start()
    return copies


def gate_up(masks, info, parts, gate, up, arrived):
    count, depth = parts[0].shape
    rows = len(parts) * count
    blocks, pieces = len(parts), len(arrived)
    width = arrived[0].shape[1]

    def body(info_ref, *refs):
        part_refs, refs = refs[:blocks], refs[blocks:]
        wholes, refs = refs[:2], refs[2:]
        piece_refs, refs = refs[:pieces], refs[pieces:]
        act_refs, (x, held, sems) = refs[:-3], refs[-3:]
        copies = load_pieces(masks, info_ref, wholes, piece_refs, held, sems)
        for at, block in enumerate(part_refs):
            x[pl.ds(at * count, count), :] = block[...]
        for copy in copies:
            copy.wait()
        for at in range(0, width, TILE):
            g = jnp.dot(x[...], held[0, :, at : at + TILE], preferred_element_type=jnp.float32)
            u = jnp.dot(x[...], held[1, :, at : at + TILE], preferred_element_type=jnp.float32)
            act = (g / (1.0 + jnp.exp(-g)) * u).astype(jnp.bfloat16)
            for group, act_ref in enumerate(act_refs):
                act_ref[:, at : at + TILE] = act[group * 4 * count : (group + 1) * 4 * count]

    return pl.pallas_call(
        body,
        in_specs=[smem()] + [vmem()] * blocks + [anywhere()] * (2 + pieces),
        out_specs=[vmem()] * (blocks // 4),
        out_shape=[jax.ShapeDtypeStruct((4 * count, width), jnp.bfloat16)] * (blocks // 4),
        scratch_shapes=[
            pltpu.VMEM((rows, depth), jnp.bfloat16),
            pltpu.VMEM((2, depth, width), jnp.bfloat16),
            pltpu.SemaphoreType.DMA((pieces + 1, 2)),
        ],
        compiler_params=params(),
        cost_estimate=cost(False),
    )(info, *parts, gate, up, *arrived)


def down_rows(masks, info, acts, down, arrived, gate=False):
    rows, width = acts[0].shape
    groups, pieces = len(acts), len(arrived)
    depth = arrived[0].shape[0] * len(masks)

    def body(info_ref, *refs):
        act_refs, down_ref, refs = refs[:groups], refs[groups], refs[groups + 1 :]
        piece_refs, outs, (held, sems) = refs[:pieces], refs[pieces:-2], refs[-2:]
        for copy in load_pieces(masks, info_ref, [down_ref], piece_refs, held, sems):
            copy.wait()
        for group, act in enumerate(act_refs):
            for at in range(0, depth, TILE):
                part = lax.dot_general(
                    act[...],
                    held[0, at : at + TILE, :],
                    (((1,), (1,)), ((), ())),
                    preferred_element_type=jnp.float32,
                )
                split_rows(part, at, outs[4 * group : 4 * group + 4])

    sums = pl.pallas_call(
        body,
        in_specs=[smem()] + [vmem()] * groups + [anywhere()] * (1 + pieces),
        out_specs=[vmem()] * (4 * groups),
        out_shape=split_shapes(rows, depth) * groups,
        scratch_shapes=[
            pltpu.VMEM((1, depth, width), jnp.bfloat16),
            pltpu.SemaphoreType.DMA((pieces + 1, 1)),
        ],
        compiler_params=params(),
        cost_estimate=cost(gate),
    )(info, *acts, down, *arrived)
    return [sums[4 * at : 4 * at + 4] for at in range(groups)]


def gather_rows(rows, across=None):
    if across is None:
        across = swap(rows, "mp", 2)
    return [rows, swap(rows, "mp", 1), across, swap(across, "mp", 1)]


def reduce_rows(own, across, far_own, far_across):
    sent = (across + swap(far_across, "mp", 1).astype(jnp.float32)).astype(jnp.bfloat16)
    return (own, swap(far_own, "mp", 1)), swap(sent, "mp", 2), sent


def total(kept, came):
    own, other = kept
    return own + other.astype(jnp.float32) + came.astype(jnp.float32)


def after(value, *earlier):
    return lax.optimization_barrier((value,) + earlier)[0] if earlier else value


def without(held, mask):
    return {at: piece for at, piece in held.items() if at != mask}


def join(*values):
    return lax.optimization_barrier(values)


def over_bits(held, bits):
    for bit in bits:
        held.update({mask ^ bit: swap(piece, "dp", bit) for mask, piece in list(held.items())})
    return held


def facts_body(info, lengths, requests, frequency, cosine, sine, of_row, of_column):
    rows = requests.shape[1]
    member, source = info[MEMBER], info[SOURCE]

    def places(size, axis, shape):
        at = lax.broadcasted_iota(jnp.int32, shape, axis)
        step = size // 4
        block = sum((at >= edge).astype(jnp.int32) for edge in (step, 2 * step, 3 * step))
        return at + ((member ^ block) - block) * step

    place = places(rows, 0, (rows, 1))
    request = requests[...]
    first, low = jnp.zeros_like(place), jnp.zeros_like(place)
    begin = lengths[source, 0]
    length = jnp.zeros_like(place) + begin
    for label in range(1, lengths.shape[1]):
        start = jnp.sum((request < label).astype(jnp.int32), axis=1, keepdims=True)
        reached = place >= start
        first = jnp.where(reached, start, first)
        low = jnp.where(reached, begin, low)
        length = jnp.where(reached, lengths[source, label], length)
        begin = begin + lengths[source, label]
    angle = (length + place - first).astype(jnp.float32) * frequency[...]
    cosine[...] = jnp.cos(angle)
    lane = lax.broadcasted_iota(jnp.int32, (1, HEAD_DIM), 1)
    sine[...] = jnp.sin(angle) * jnp.where(lane < HEAD_DIM // 2, -1.0, 1.0)
    column = lax.broadcasted_iota(jnp.int32, of_row.shape, 1)
    of_row[...] = jnp.where(
        column == 0, low, jnp.where(column == 1, low + length, jnp.where(column == 2, first, place))
    )
    of_column[0:1, :] = places(of_column.shape[1], 1, (1, of_column.shape[1]))
    of_column[1:2, :] = places(rows, 1, (1, of_column.shape[1]))


def row_facts(info, lengths, requests, cached):
    rows = requests.shape[1]
    half = HEAD_DIM // 2
    frequency = ROPE_BASE ** (-np.arange(half, dtype=np.float32) / np.float32(half))
    frequency = jnp.asarray(np.concatenate([frequency, frequency])[None], jnp.float32)
    turn = jax.ShapeDtypeStruct((rows, HEAD_DIM), jnp.float32)
    return pl.pallas_call(
        facts_body,
        in_specs=[smem(), smem(), vmem(), vmem()],
        out_specs=[vmem()] * 4,
        out_shape=[
            turn,
            turn,
            jax.ShapeDtypeStruct((rows, 8), jnp.int32),
            jax.ShapeDtypeStruct((8, cached), jnp.int32),
        ],
        compiler_params=params(),
        cost_estimate=cost(False),
    )(info, lengths, requests, frequency)


def local(
    tokens,
    request_ids,
    cache_entries,
    cached_lengths,
    traded,
    query_weight,
    key_weight,
    value_weight,
    output_weight,
    gate_weight,
    up_weight,
    down_weight,
):
    replica = lax.axis_index("rep")
    within = lax.axis_index("dp")
    member = lax.axis_index("mp")
    planes = lax.axis_size("dp")
    pair = planes // 2
    bits = [1 << at for at in range(planes.bit_length() - 1) if 1 << at != pair]
    place = (within // pair) % 2
    mine, leaving = 2 * place + replica, 2 * (1 - place) + replica
    source = jnp.where(traded[0] == 1, 1 - replica, replica) * planes + within
    info = jnp.stack([member, within, mine, leaving, source]).astype(jnp.int32)

    *normed, blocks_0, blocks_1, blocks_2, blocks_3, wide_leaving, wide_mine = prepare(
        info, tokens, cache_entries, gate_weight, up_weight
    )
    blocks = [blocks_0, swap(blocks_1, "mp", 1), swap(blocks_2, "mp", 2), swap(blocks_3, "mp", 3)]
    facts = row_facts(info, cached_lengths, request_ids, 4 * cache_entries.shape[0])
    came = [swap(block, "rep", 1) for block in blocks]
    over_chip = [swap(half, "mp", 2) for half in normed]
    over_chip, came[0], came[1] = join(over_chip, came[0], came[1])
    parts = [gather_rows(*halves) for halves in zip(normed, over_chip)]
    parts = [half for pair_of in zip(*parts) for half in pair_of]

    def near_side(piece):
        return without(over_bits({0: piece}, bits), 0)

    def across(piece):
        return {pair: swap(piece, "dp", pair)}

    def far_side(held):
        return without(over_bits(dict(held), bits), pair)

    wide = {**across(wide_leaving), **near_side(after(wide_mine, blocks[1]))}

    q, k, v = project(parts, facts[0], facts[1], query_weight, key_weight, value_weight)
    came, q = join(came, q)
    sums = attend(traded, q, k, v, blocks, came, facts[2], facts[3], output_weight)
    sums, wide = join(sums, wide)
    kept, came, sent = reduce_rows(*sums)
    down_cut = cut(info, after(down_weight, sent))
    kept, came, down_cut = join(kept, came, down_cut)
    wide.update(far_side({pair: wide[pair]}))
    state_own = (tokens.astype(jnp.float32) + total(kept, came)).astype(jnp.bfloat16)
    normed_own = layer_norm(state_own.astype(jnp.float32)).astype(jnp.bfloat16)

    rows_z = swap(normed_own, "dp", pair)
    rows_x = swap(normed_own, "rep", 1)
    over_chip = swap(normed_own, "mp", 2), swap(rows_x, "mp", 2)
    rows_z, wide, over_chip = join(rows_z, wide, over_chip)
    parts = gather_rows(normed_own, over_chip[0]) + gather_rows(rows_x, over_chip[1])
    rows_both = swap(rows_z, "rep", 1)
    back = {**across(after(down_cut[0], rows_z)), **near_side(after(down_cut[1], rows_z))}
    parts += gather_rows(rows_z)
    masks = [0] + list(wide)
    in_order = lambda held: [held[mask] for mask in masks[1:]]
    acts = gate_up(masks, info, parts, gate_weight, up_weight, in_order(wide))
    parts = gather_rows(rows_both)
    parts[0] = after(parts[0], acts[0])
    acts, back = join(acts, back)
    back.update(far_side({pair: back[pair]}))
    acts += gate_up(masks, info, parts, gate_weight, up_weight, in_order(wide))

    def sums_of(*groups, gate=False):
        return down_rows(masks, info, groups, down_weight, in_order(back), gate)

    def crossed(value, axis, mask):
        return swap(value.astype(jnp.bfloat16), axis, mask).astype(jnp.float32)

    found_both, found_z = sums_of(acts[3], acts[2])
    kept, came, sent = reduce_rows(*found_both)
    kept_z, came_z, sent_z = reduce_rows(*found_z)
    found_x, found = sums_of(after(acts[1], sent, sent_z), acts[0], gate=True)
    came, found_x, found = join(came, found_x, found)
    of_both, of_z = total(kept, came), total(kept_z, came_z)
    of_both = of_both.astype(jnp.bfloat16)
    sent = (of_z + crossed(of_both, "rep", 1)).astype(jnp.bfloat16)
    of_z = swap(sent, "dp", pair).astype(jnp.float32)
    found_x, found = after((found_x, found), of_both)
    kept, came, sent_x = reduce_rows(*found_x)
    of_x = total(kept, came)
    of_own = total(*reduce_rows(*after(found, sent_x))[:2])
    of_x = after(of_x, sent)
    columns = of_x.shape[1]
    of_x = [crossed(of_x[:, at : at + columns // 2], "rep", 1) for at in (0, columns // 2)]
    of_own = of_own + jnp.concatenate(of_x, axis=1)
    return (state_own.astype(jnp.float32) + (of_own + of_z)).astype(jnp.bfloat16)


def solution(mesh):
    in_specs = (
        P(("rep", "dp", "mp"), None),
        P(("rep", "dp"), None),
        P(("rep", "dp", "mp"), None),
        P(),
        P("dp"),
        P(None, "mp"),
        P(None, "mp"),
        P(None, "mp"),
        P("mp", None),
        P("dp", "mp"),
        P("dp", "mp"),
        P("dp", "mp"),
    )
    out_specs = P(("rep", "dp", "mp"), None)
    return jax.shard_map(local, mesh=mesh, in_specs=in_specs, out_specs=out_specs, check_vma=False)
```

```python
import math

import jax
import jax.numpy as jnp
import numpy as np
from jax import lax
from jax.experimental import pallas as pl
from jax.experimental.pallas import tpu as pltpu
from jax.sharding import PartitionSpec as P

HEAD_DIM = 128
EPSILON = 1e-05
ROPE_BASE = 10000.0
VMEM_LIMIT = 28 * 1024 * 1024
VMEM_WHOLE = 60 * 1024 * 1024
TILE = 256
MASKED = -1e30
MEMBER, WITHIN, MINE, LEAVING, SOURCE = range(5)


def swap(value, axis, mask):
    pairs = [(source, source ^ mask) for source in range(lax.axis_size(axis))]
    return lax.ppermute(value, axis, pairs)


def layer_norm(rows):
    center = rows - jnp.mean(rows, axis=-1, keepdims=True)
    spread = jnp.mean(center * center, axis=-1, keepdims=True)
    return center * lax.rsqrt(spread + EPSILON)


def vmem():
    return pl.BlockSpec(memory_space=pltpu.VMEM)


def smem():
    return pl.BlockSpec(memory_space=pltpu.SMEM)


def anywhere():
    return pl.BlockSpec(memory_space=pl.ANY)


def params(limit=VMEM_LIMIT):
    return pltpu.CompilerParams(vmem_limit_bytes=limit)


def cost(gate=True):
    return pl.CostEstimate(flops=10**11 if gate else 0, bytes_accessed=0, transcendentals=0)


def prepare(info, tokens, entries, *weights):
    rows, columns = entries.shape
    stack, depth, width = len(weights), weights[0].shape[0], weights[0].shape[1] // 4

    def body(info_ref, token_ref, entry_ref, *refs):
        sources, normed, blocks = refs[:stack], refs[stack : stack + 2], refs[stack + 2 : stack + 6]
        outs, sems = refs[stack + 6 : -1], refs[-1]
        copies = cut_copies(info_ref, sources, outs, sems)
        part = blocks[0].shape[1] // 2
        for mask, out in enumerate(blocks):
            begin = pl.multiple_of((info_ref[MEMBER] ^ mask) * part, part)
            out[:, :part] = entry_ref[:, pl.ds(begin, part)]
            out[:, part:] = entry_ref[:, pl.ds(4 * part + begin, part)]
        found = layer_norm(token_ref[...].astype(jnp.float32)).astype(jnp.bfloat16)
        for half, out in enumerate(normed):
            out[...] = found[:, half * out.shape[1] : (half + 1) * out.shape[1]]
        for copy in copies:
            copy.wait()

    return pl.pallas_call(
        body,
        in_specs=[smem(), vmem(), vmem()] + [anywhere()] * stack,
        out_specs=[vmem()] * 8,
        out_shape=[jax.ShapeDtypeStruct((tokens.shape[0], tokens.shape[1] // 2), jnp.bfloat16)] * 2
        + [jax.ShapeDtypeStruct((rows, columns // 4), jnp.bfloat16)] * 4
        + [jax.ShapeDtypeStruct((stack * depth, width), jnp.bfloat16)] * 2,
        scratch_shapes=[pltpu.SemaphoreType.DMA((2, stack))],
        compiler_params=params(VMEM_WHOLE),
        cost_estimate=cost(False),
    )(info, tokens, entries, *weights)


def cut_copies(info, sources, outs, sems):
    rows = sources[0].shape[0]
    width = outs[0].shape[1]
    copies = []
    for at, out in enumerate(outs):
        there = pl.ds(pl.multiple_of(info[(LEAVING, MINE)[at]] * width, width), width)
        for which, source in enumerate(sources):
            place = out.at[pl.ds(which * rows, rows), :]
            copies.append(pltpu.make_async_copy(source.at[:, there], place, sems.at[at, which]))
    for copy in copies:
        copy.start()
    return copies


def cut(info, *weights):
    rows, columns = weights[0].shape
    width = columns // 4
    count, stack = 2, len(weights)

    def body(info_ref, *refs):
        for copy in cut_copies(info_ref, refs[:stack], refs[stack:-1], refs[-1]):
            copy.wait()

    return pl.pallas_call(
        body,
        in_specs=[smem()] + [anywhere()] * stack,
        out_specs=[vmem()] * count,
        out_shape=[jax.ShapeDtypeStruct((stack * rows, width), jnp.bfloat16)] * count,
        scratch_shapes=[pltpu.SemaphoreType.DMA((count, stack))],
        compiler_params=params(),
        cost_estimate=cost(False),
    )(info, *weights)


def project_body(*refs):
    parts, refs = refs[:8], refs[8:]
    cosine, sine, wq, wk, wv, q_ref, k_ref, v_ref, rows = refs
    count, half = parts[0].shape

    @pl.when(pl.program_id(0) == 0)
    def _():
        for at, part in enumerate(parts):
            begin = at % 2 * half
            rows[pl.ds(at // 2 * count, count), begin : begin + half] = part[...]

    x = rows[...]
    width = wq.shape[1]
    for weight, out, turned in ((wq, q_ref, True), (wk, k_ref, True), (wv, v_ref, False)):
        product = jnp.dot(x, weight[...], preferred_element_type=jnp.float32)
        if not turned:
            out[...] = product.astype(jnp.bfloat16)
            continue
        for at in range(0, width, HEAD_DIM):
            head = product[:, at : at + HEAD_DIM]
            other = pltpu.roll(head, HEAD_DIM // 2, 1)
            out[:, at : at + HEAD_DIM] = (head * cosine[...] + other * sine[...]).astype(
                jnp.bfloat16
            )


def project(parts, cosine, sine, wq, wk, wv):
    count, depth = parts[0].shape[0], 2 * parts[0].shape[1]
    rows, width = 4 * count, wq.shape[1]
    whole = lambda shape: pl.BlockSpec(shape, lambda i: (0, 0))
    column = pl.BlockSpec((depth, TILE), lambda i: (0, i))
    out = pl.BlockSpec((rows, TILE), lambda i: (0, i))
    shape = jax.ShapeDtypeStruct((rows, width), jnp.bfloat16)
    return pl.pallas_call(
        project_body,
        grid=(width // TILE,),
        in_specs=[whole((count, depth // 2))] * 8 + [whole((rows, HEAD_DIM))] * 2 + [column] * 3,
        out_specs=[out] * 3,
        out_shape=[shape] * 3,
        scratch_shapes=[pltpu.VMEM((rows, depth), jnp.bfloat16)],
        compiler_params=params(),
        cost_estimate=cost(False),
    )(*parts, cosine, sine, wq, wk, wv)


def attend_body(traded, q, k, v, *refs):
    own, came, refs = refs[:4], refs[4:8], refs[8:]
    of_row, of_column, wo, refs = refs[0], refs[1], refs[2], refs[3:]
    outs, (mixed, cached, weight, sems) = refs[:-4], refs[-4:]
    load = pltpu.make_async_copy(wo, weight, sems.at[4])
    count = own[0].shape[0]

    def fetch(blocks):
        copies = [
            pltpu.make_async_copy(block, cached.at[pl.ds(at * count, count), :], sems.at[at])
            for at, block in enumerate(blocks)
        ]
        for copy in copies:
            copy.start()
        load.start()
        for copy in copies:
            copy.wait()

    @pl.when(traded[0] == 1)
    def _():
        fetch(came)

    @pl.when(traded[0] != 1)
    def _():
        fetch(own)

    rows, width = q.shape
    heads = width // HEAD_DIM
    low, high = of_row[:, 0:1], of_row[:, 1:2]
    first, place = of_row[:, 2:3], of_row[:, 3:4]
    column = of_column[0:1, :]
    fresh = of_column[1:2, :rows]
    on_cached = (column >= low) & (column < high)
    on_fresh = (fresh >= first) & (fresh <= place)
    scale = 1.0 / math.sqrt(HEAD_DIM)
    contract_last = (((1,), (1,)), ((), ()))
    for head in range(heads):
        at = slice(head * HEAD_DIM, (head + 1) * HEAD_DIM)
        after = slice(width + head * HEAD_DIM, width + (head + 1) * HEAD_DIM)
        query = q[:, at]
        old = lax.dot_general(
            query, cached[:, at], contract_last, preferred_element_type=jnp.float32
        )
        new = lax.dot_general(query, k[:, at], contract_last, preferred_element_type=jnp.float32)
        old = jnp.where(on_cached, old * scale, MASKED)
        new = jnp.where(on_fresh, new * scale, MASKED)
        top = jnp.maximum(
            jnp.max(old, axis=-1, keepdims=True), jnp.max(new, axis=-1, keepdims=True)
        )
        old = jnp.exp(old - top)
        new = jnp.exp(new - top)
        share = 1.0 / (jnp.sum(old, axis=-1, keepdims=True) + jnp.sum(new, axis=-1, keepdims=True))
        sums = jnp.dot(
            (old * share).astype(jnp.bfloat16), cached[:, after], preferred_element_type=jnp.float32
        ) + jnp.dot(
            (new * share).astype(jnp.bfloat16), v[:, at], preferred_element_type=jnp.float32
        )
        mixed[:, at] = sums.astype(jnp.bfloat16)
    load.wait()
    left = mixed[...]
    for at in range(0, weight.shape[1], TILE):
        part = jnp.dot(left, weight[:, at : at + TILE], preferred_element_type=jnp.float32)
        split_rows(part, at, outs)


def split_rows(part, at, outs):
    count = part.shape[0] // 4
    for out, block in zip(outs, (0, 2, 1, 3)):
        rows = part[block * count : (block + 1) * count]
        out[:, at : at + TILE] = rows.astype(out.dtype)


def split_shapes(rows, depth):
    return [
        jax.ShapeDtypeStruct((rows // 4, depth), kind)
        for kind in (jnp.float32, jnp.float32, jnp.bfloat16, jnp.bfloat16)
    ]


def attend(traded, q, k, v, own, came, of_row, of_column, wo):
    rows, width = q.shape
    depth = wo.shape[1]
    cached = of_column.shape[1]
    keys = cached + rows
    return pl.pallas_call(
        attend_body,
        in_specs=[smem()] + [vmem()] * 3 + [anywhere()] * 8 + [vmem()] * 2 + [anywhere()],
        out_specs=[vmem()] * 4,
        out_shape=split_shapes(rows, depth),
        scratch_shapes=[
            pltpu.VMEM((rows, width), jnp.bfloat16),
            pltpu.VMEM((cached, 2 * width), jnp.bfloat16),
            pltpu.VMEM(wo.shape, jnp.bfloat16),
            pltpu.SemaphoreType.DMA((5,)),
        ],
        compiler_params=params(),
        cost_estimate=cost(False),
    )(traded, q, k, v, *own, *came, of_row, of_column, wo)


def load_pieces(masks, info, wholes, pieces, held, sems):
    shard, width = wholes[0].shape[0], pieces[0].shape[1]
    columns = pl.ds(pl.multiple_of(info[MINE] * width, width), width)
    copies = []
    for at, mask in enumerate(masks):
        there = pl.ds(pl.multiple_of((info[WITHIN] ^ mask) * shard, shard), shard)
        for which, whole in enumerate(wholes):
            source = pieces[at - 1].at[pl.ds(which * shard, shard), :] if at else whole.at[:, columns]
            place = held.at[which, there, :]
            copies.append(pltpu.make_async_copy(source, place, sems.at[at, which]))
    for copy in copies:
        copy.start()
    return copies


def gate_up(masks, info, parts, gate, up, arrived):
    count, depth = parts[0].shape
    rows = len(parts) * count
    blocks, pieces = len(parts), len(arrived)
    width = arrived[0].shape[1]

    def body(info_ref, *refs):
        part_refs, refs = refs[:blocks], refs[blocks:]
        wholes, refs = refs[:2], refs[2:]
        piece_refs, refs = refs[:pieces], refs[pieces:]
        act_refs, (x, held, sems) = refs[:-3], refs[-3:]
        copies = load_pieces(masks, info_ref, wholes, piece_refs, held, sems)
        for at, block in enumerate(part_refs):
            x[pl.ds(at * count, count), :] = block[...]
        for copy in copies:
            copy.wait()
        for at in range(0, width, TILE):
            g = jnp.dot(x[...], held[0, :, at : at + TILE], preferred_element_type=jnp.float32)
            u = jnp.dot(x[...], held[1, :, at : at + TILE], preferred_element_type=jnp.float32)
            act = (g / (1.0 + jnp.exp(-g)) * u).astype(jnp.bfloat16)
            for group, act_ref in enumerate(act_refs):
                act_ref[:, at : at + TILE] = act[group * 4 * count : (group + 1) * 4 * count]

    return pl.pallas_call(
        body,
        in_specs=[smem()] + [vmem()] * blocks + [anywhere()] * (2 + pieces),
        out_specs=[vmem()] * (blocks // 4),
        out_shape=[jax.ShapeDtypeStruct((4 * count, width), jnp.bfloat16)] * (blocks // 4),
        scratch_shapes=[
            pltpu.VMEM((rows, depth), jnp.bfloat16),
            pltpu.VMEM((2, depth, width), jnp.bfloat16),
            pltpu.SemaphoreType.DMA((pieces + 1, 2)),
        ],
        compiler_params=params(),
        cost_estimate=cost(False),
    )(info, *parts, gate, up, *arrived)


def down_rows(masks, info, acts, down, arrived, gate=False):
    rows, width = acts[0].shape
    groups, pieces = len(acts), len(arrived)
    depth = arrived[0].shape[0] * len(masks)

    def body(info_ref, *refs):
        act_refs, down_ref, refs = refs[:groups], refs[groups], refs[groups + 1 :]
        piece_refs, outs, (held, sems) = refs[:pieces], refs[pieces:-2], refs[-2:]
        for copy in load_pieces(masks, info_ref, [down_ref], piece_refs, held, sems):
            copy.wait()
        for group, act in enumerate(act_refs):
            for at in range(0, depth, TILE):
                part = lax.dot_general(
                    act[...],
                    held[0, at : at + TILE, :],
                    (((1,), (1,)), ((), ())),
                    preferred_element_type=jnp.float32,
                )
                split_rows(part, at, outs[4 * group : 4 * group + 4])

    sums = pl.pallas_call(
        body,
        in_specs=[smem()] + [vmem()] * groups + [anywhere()] * (1 + pieces),
        out_specs=[vmem()] * (4 * groups),
        out_shape=split_shapes(rows, depth) * groups,
        scratch_shapes=[
            pltpu.VMEM((1, depth, width), jnp.bfloat16),
            pltpu.SemaphoreType.DMA((pieces + 1, 1)),
        ],
        compiler_params=params(),
        cost_estimate=cost(gate),
    )(info, *acts, down, *arrived)
    return [sums[4 * at : 4 * at + 4] for at in range(groups)]


def gather_rows(rows, across=None):
    if across is None:
        across = swap(rows, "mp", 2)
    return [rows, swap(rows, "mp", 1), across, swap(across, "mp", 1)]


def reduce_rows(own, across, far_own, far_across, edges=()):
    came = swap(far_across, "mp", 1)
    bounds = [0, *edges, own.shape[1]]
    sent = [
        (across[:, begin:end] + came[:, begin:end].astype(jnp.float32)).astype(jnp.bfloat16)
        for begin, end in zip(bounds, bounds[1:])
    ]
    other = swap(far_own, "mp", 1)
    kept = [(own[:, begin:end], other[:, begin:end]) for begin, end in zip(bounds, bounds[1:])]
    return kept, [swap(part, "mp", 2) for part in sent], sent


def total(kept, came):
    own, other = kept
    return own + other.astype(jnp.float32) + came.astype(jnp.float32)


def after(value, *earlier):
    return lax.optimization_barrier((value,) + earlier)[0] if earlier else value


def without(held, mask):
    return {at: piece for at, piece in held.items() if at != mask}


def join(*values):
    return lax.optimization_barrier(values)


def over_bits(held, bits):
    for bit in bits:
        held.update({mask ^ bit: swap(piece, "dp", bit) for mask, piece in list(held.items())})
    return held


def facts_body(info, lengths, requests, frequency, cosine, sine, of_row, of_column):
    rows = requests.shape[1]
    member, source = info[MEMBER], info[SOURCE]

    def places(size, axis, shape):
        at = lax.broadcasted_iota(jnp.int32, shape, axis)
        step = size // 4
        block = sum((at >= edge).astype(jnp.int32) for edge in (step, 2 * step, 3 * step))
        return at + ((member ^ block) - block) * step

    place = places(rows, 0, (rows, 1))
    request = requests[...]
    first, low = jnp.zeros_like(place), jnp.zeros_like(place)
    begin = lengths[source, 0]
    length = jnp.zeros_like(place) + begin
    for label in range(1, lengths.shape[1]):
        start = jnp.sum((request < label).astype(jnp.int32), axis=1, keepdims=True)
        reached = place >= start
        first = jnp.where(reached, start, first)
        low = jnp.where(reached, begin, low)
        length = jnp.where(reached, lengths[source, label], length)
        begin = begin + lengths[source, label]
    angle = (length + place - first).astype(jnp.float32) * frequency[...]
    cosine[...] = jnp.cos(angle)
    lane = lax.broadcasted_iota(jnp.int32, (1, HEAD_DIM), 1)
    sine[...] = jnp.sin(angle) * jnp.where(lane < HEAD_DIM // 2, -1.0, 1.0)
    column = lax.broadcasted_iota(jnp.int32, of_row.shape, 1)
    of_row[...] = jnp.where(
        column == 0, low, jnp.where(column == 1, low + length, jnp.where(column == 2, first, place))
    )
    of_column[0:1, :] = places(of_column.shape[1], 1, (1, of_column.shape[1]))
    of_column[1:2, :] = places(rows, 1, (1, of_column.shape[1]))


def row_facts(info, lengths, requests, cached):
    rows = requests.shape[1]
    half = HEAD_DIM // 2
    frequency = ROPE_BASE ** (-np.arange(half, dtype=np.float32) / np.float32(half))
    frequency = jnp.asarray(np.concatenate([frequency, frequency])[None], jnp.float32)
    turn = jax.ShapeDtypeStruct((rows, HEAD_DIM), jnp.float32)
    return pl.pallas_call(
        facts_body,
        in_specs=[smem(), smem(), vmem(), vmem()],
        out_specs=[vmem()] * 4,
        out_shape=[
            turn,
            turn,
            jax.ShapeDtypeStruct((rows, 8), jnp.int32),
            jax.ShapeDtypeStruct((8, cached), jnp.int32),
        ],
        compiler_params=params(),
        cost_estimate=cost(False),
    )(info, lengths, requests, frequency)


def local(
    tokens,
    request_ids,
    cache_entries,
    cached_lengths,
    traded,
    query_weight,
    key_weight,
    value_weight,
    output_weight,
    gate_weight,
    up_weight,
    down_weight,
):
    replica = lax.axis_index("rep")
    within = lax.axis_index("dp")
    member = lax.axis_index("mp")
    planes = lax.axis_size("dp")
    pair = planes // 2
    bits = [1 << at for at in range(planes.bit_length() - 1) if 1 << at != pair]
    place = (within // pair) % 2
    mine, leaving = 2 * place + replica, 2 * (1 - place) + replica
    source = jnp.where(traded[0] == 1, 1 - replica, replica) * planes + within
    info = jnp.stack([member, within, mine, leaving, source]).astype(jnp.int32)

    *normed, blocks_0, blocks_1, blocks_2, blocks_3, wide_leaving, wide_mine = prepare(
        info, tokens, cache_entries, gate_weight, up_weight
    )
    blocks = [blocks_0, swap(blocks_1, "mp", 1), swap(blocks_2, "mp", 2), swap(blocks_3, "mp", 3)]
    facts = row_facts(info, cached_lengths, request_ids, 4 * cache_entries.shape[0])
    came = [swap(block, "rep", 1) for block in blocks]
    over_chip = [swap(half, "mp", 2) for half in normed]
    over_chip, came[0], came[1] = join(over_chip, came[0], came[1])
    parts = [gather_rows(*halves) for halves in zip(normed, over_chip)]
    parts = [half for pair_of in zip(*parts) for half in pair_of]

    def near_side(piece):
        return without(over_bits({0: piece}, bits), 0)

    def across(piece):
        return {pair: swap(piece, "dp", pair)}

    def far_side(held):
        return without(over_bits(dict(held), bits), pair)

    wide = {**across(wide_leaving), **near_side(after(wide_mine, blocks[1]))}

    q, k, v = project(parts, facts[0], facts[1], query_weight, key_weight, value_weight)
    came, q = join(came, q)
    sums = attend(traded, q, k, v, blocks, came, facts[2], facts[3], output_weight)
    sums, wide = join(sums, wide)
    (kept,), (came,), (sent,) = reduce_rows(*sums)
    down_cut = cut(info, after(down_weight, sent))
    kept, came, down_cut = join(kept, came, down_cut)
    wide.update(far_side({pair: wide[pair]}))
    state_own = (tokens.astype(jnp.float32) + total(kept, came)).astype(jnp.bfloat16)
    normed_own = layer_norm(state_own.astype(jnp.float32)).astype(jnp.bfloat16)

    rows_z = swap(normed_own, "dp", pair)
    rows_x = swap(normed_own, "rep", 1)
    over_chip = swap(normed_own, "mp", 2), swap(rows_x, "mp", 2)
    rows_z, wide, over_chip = join(rows_z, wide, over_chip)
    parts = gather_rows(normed_own, over_chip[0]) + gather_rows(rows_x, over_chip[1])
    rows_both = swap(rows_z, "rep", 1)
    rows_z = gather_rows(rows_z)
    back = {**across(after(down_cut[0], rows_z[0])), **near_side(after(down_cut[1], rows_z[1]))}
    parts += rows_z
    masks = [0] + list(wide)
    in_order = lambda held: [held[mask] for mask in masks[1:]]
    acts = gate_up(masks, info, parts, gate_weight, up_weight, in_order(wide))
    parts = gather_rows(rows_both)
    parts[0] = after(parts[0], acts[0])
    acts, back = join(acts, back)
    back.update(far_side({pair: back[pair]}))
    acts += gate_up(masks, info, parts, gate_weight, up_weight, in_order(wide))

    def sums_of(*groups, gate=False):
        return down_rows(masks, info, groups, down_weight, in_order(back), gate)

    def crossed(value, axis, mask):
        return swap(value.astype(jnp.bfloat16), axis, mask).astype(jnp.float32)

    edges = (tokens.shape[1] * 5 // 8,)
    found_both, found_z = sums_of(acts[3], acts[2])
    kept, came, sent = reduce_rows(*found_both, edges)
    kept_z, came_z, sent_z = reduce_rows(*found_z, edges)
    found_x, found = sums_of(after(acts[1], *sent, *sent_z), acts[0], gate=True)
    came[0], found_x, found = join(came[0], found_x, found)
    of_both = [total(*terms).astype(jnp.bfloat16) for terms in zip(kept, came)]
    of_z = [total(*terms) for terms in zip(kept_z, came_z)]
    sent = [
        (part + crossed(more, "rep", 1)).astype(jnp.bfloat16) for part, more in zip(of_z, of_both)
    ]
    of_z = jnp.concatenate([swap(part, "dp", pair) for part in sent], axis=1).astype(jnp.float32)
    found_x, found = after((found_x, found), *of_both)
    (kept,), (came,), sent_x = reduce_rows(*found_x)
    of_x = total(kept, came)
    (kept,), (came,), _ = reduce_rows(*after(found, *sent_x))
    of_own = total(kept, came)
    of_x = after(of_x, *sent)
    columns = of_x.shape[1]
    of_x = [crossed(of_x[:, at : at + columns // 2], "rep", 1) for at in (0, columns // 2)]
    of_own = of_own + jnp.concatenate(of_x, axis=1)
    return (state_own.astype(jnp.float32) + (of_own + of_z)).astype(jnp.bfloat16)


def solution(mesh):
    in_specs = (
        P(("rep", "dp", "mp"), None),
        P(("rep", "dp"), None),
        P(("rep", "dp", "mp"), None),
        P(),
        P("dp"),
        P(None, "mp"),
        P(None, "mp"),
        P(None, "mp"),
        P("mp", None),
        P("dp", "mp"),
        P("dp", "mp"),
        P("dp", "mp"),
    )
    out_specs = P(("rep", "dp", "mp"), None)
    return jax.shard_map(local, mesh=mesh, in_specs=in_specs, out_specs=out_specs, check_vma=False)
```

```python
import math

import jax
import jax.numpy as jnp
import numpy as np
from jax import lax
from jax.experimental import pallas as pl
from jax.experimental.pallas import tpu as pltpu
from jax.sharding import PartitionSpec as P

HEAD_DIM = 128
EPSILON = 1e-05
ROPE_BASE = 10000.0
VMEM_LIMIT = 28 * 1024 * 1024
VMEM_WHOLE = 60 * 1024 * 1024
TILE = 256
MASKED = -1e30
MEMBER, WITHIN, MINE, LEAVING, SOURCE = range(5)


def swap(value, axis, mask):
    pairs = [(source, source ^ mask) for source in range(lax.axis_size(axis))]
    return lax.ppermute(value, axis, pairs)


def layer_norm(rows):
    center = rows - jnp.mean(rows, axis=-1, keepdims=True)
    spread = jnp.mean(center * center, axis=-1, keepdims=True)
    return center * lax.rsqrt(spread + EPSILON)


def vmem():
    return pl.BlockSpec(memory_space=pltpu.VMEM)


def smem():
    return pl.BlockSpec(memory_space=pltpu.SMEM)


def anywhere():
    return pl.BlockSpec(memory_space=pl.ANY)


def params(limit=VMEM_LIMIT):
    return pltpu.CompilerParams(vmem_limit_bytes=limit)


def cost(gate=True):
    return pl.CostEstimate(flops=10**11 if gate else 0, bytes_accessed=0, transcendentals=0)


def prepare(info, tokens, entries, *weights):
    rows, columns = entries.shape
    stack, depth, width = len(weights), weights[0].shape[0], weights[0].shape[1] // 4

    def body(info_ref, token_ref, entry_ref, *refs):
        sources, normed, blocks = refs[:stack], refs[stack : stack + 2], refs[stack + 2 : stack + 6]
        outs, sems = refs[stack + 6 : -1], refs[-1]
        copies = cut_copies(info_ref, sources, outs, sems)
        part = blocks[0].shape[1] // 2
        for mask, out in enumerate(blocks):
            begin = pl.multiple_of((info_ref[MEMBER] ^ mask) * part, part)
            out[:, :part] = entry_ref[:, pl.ds(begin, part)]
            out[:, part:] = entry_ref[:, pl.ds(4 * part + begin, part)]
        found = layer_norm(token_ref[...].astype(jnp.float32)).astype(jnp.bfloat16)
        for half, out in enumerate(normed):
            out[...] = found[:, half * out.shape[1] : (half + 1) * out.shape[1]]
        for copy in copies:
            copy.wait()

    return pl.pallas_call(
        body,
        in_specs=[smem(), vmem(), vmem()] + [anywhere()] * stack,
        out_specs=[vmem()] * 8,
        out_shape=[jax.ShapeDtypeStruct((tokens.shape[0], tokens.shape[1] // 2), jnp.bfloat16)] * 2
        + [jax.ShapeDtypeStruct((rows, columns // 4), jnp.bfloat16)] * 4
        + [jax.ShapeDtypeStruct((stack * depth, width), jnp.bfloat16)] * 2,
        scratch_shapes=[pltpu.SemaphoreType.DMA((2, stack))],
        compiler_params=params(VMEM_WHOLE),
        cost_estimate=cost(False),
    )(info, tokens, entries, *weights)


def cut_copies(info, sources, outs, sems):
    rows = sources[0].shape[0]
    width = outs[0].shape[1]
    copies = []
    for at, out in enumerate(outs):
        there = pl.ds(pl.multiple_of(info[(LEAVING, MINE)[at]] * width, width), width)
        for which, source in enumerate(sources):
            place = out.at[pl.ds(which * rows, rows), :]
            copies.append(pltpu.make_async_copy(source.at[:, there], place, sems.at[at, which]))
    for copy in copies:
        copy.start()
    return copies


def cut(info, *weights):
    rows, columns = weights[0].shape
    width = columns // 4
    count, stack = 2, len(weights)

    def body(info_ref, *refs):
        for copy in cut_copies(info_ref, refs[:stack], refs[stack:-1], refs[-1]):
            copy.wait()

    return pl.pallas_call(
        body,
        in_specs=[smem()] + [anywhere()] * stack,
        out_specs=[vmem()] * count,
        out_shape=[jax.ShapeDtypeStruct((stack * rows, width), jnp.bfloat16)] * count,
        scratch_shapes=[pltpu.SemaphoreType.DMA((count, stack))],
        compiler_params=params(),
        cost_estimate=cost(False),
    )(info, *weights)


def project_body(*refs):
    parts, refs = refs[:8], refs[8:]
    cosine, sine, wq, wk, wv, q_ref, k_ref, v_ref, rows = refs
    count, half = parts[0].shape

    @pl.when(pl.program_id(0) == 0)
    def _():
        for at, part in enumerate(parts):
            begin = at % 2 * half
            rows[pl.ds(at // 2 * count, count), begin : begin + half] = part[...]

    x = rows[...]
    width = wq.shape[1]
    for weight, out, turned in ((wq, q_ref, True), (wk, k_ref, True), (wv, v_ref, False)):
        product = jnp.dot(x, weight[...], preferred_element_type=jnp.float32)
        if not turned:
            out[...] = product.astype(jnp.bfloat16)
            continue
        for at in range(0, width, HEAD_DIM):
            head = product[:, at : at + HEAD_DIM]
            other = pltpu.roll(head, HEAD_DIM // 2, 1)
            out[:, at : at + HEAD_DIM] = (head * cosine[...] + other * sine[...]).astype(
                jnp.bfloat16
            )


def project(parts, cosine, sine, wq, wk, wv):
    count, depth = parts[0].shape[0], 2 * parts[0].shape[1]
    rows, width = 4 * count, wq.shape[1]
    whole = lambda shape: pl.BlockSpec(shape, lambda i: (0, 0))
    column = pl.BlockSpec((depth, TILE), lambda i: (0, i))
    out = pl.BlockSpec((rows, TILE), lambda i: (0, i))
    shape = jax.ShapeDtypeStruct((rows, width), jnp.bfloat16)
    return pl.pallas_call(
        project_body,
        grid=(width // TILE,),
        in_specs=[whole((count, depth // 2))] * 8 + [whole((rows, HEAD_DIM))] * 2 + [column] * 3,
        out_specs=[out] * 3,
        out_shape=[shape] * 3,
        scratch_shapes=[pltpu.VMEM((rows, depth), jnp.bfloat16)],
        compiler_params=params(),
        cost_estimate=cost(False),
    )(*parts, cosine, sine, wq, wk, wv)


def attend_body(traded, q, k, v, *refs):
    own, came, refs = refs[:4], refs[4:8], refs[8:]
    of_row, of_column, wo, refs = refs[0], refs[1], refs[2], refs[3:]
    outs, (mixed, cached, weight, sems) = refs[:-4], refs[-4:]
    load = pltpu.make_async_copy(wo, weight, sems.at[4])
    count = own[0].shape[0]

    def fetch(blocks):
        copies = [
            pltpu.make_async_copy(block, cached.at[pl.ds(at * count, count), :], sems.at[at])
            for at, block in enumerate(blocks)
        ]
        for copy in copies:
            copy.start()
        load.start()
        for copy in copies:
            copy.wait()

    @pl.when(traded[0] == 1)
    def _():
        fetch(came)

    @pl.when(traded[0] != 1)
    def _():
        fetch(own)

    rows, width = q.shape
    heads = width // HEAD_DIM
    low, high = of_row[:, 0:1], of_row[:, 1:2]
    first, place = of_row[:, 2:3], of_row[:, 3:4]
    column = of_column[0:1, :]
    fresh = of_column[1:2, :rows]
    on_cached = (column >= low) & (column < high)
    on_fresh = (fresh >= first) & (fresh <= place)
    scale = 1.0 / math.sqrt(HEAD_DIM)
    contract_last = (((1,), (1,)), ((), ()))
    for head in range(heads):
        at = slice(head * HEAD_DIM, (head + 1) * HEAD_DIM)
        after = slice(width + head * HEAD_DIM, width + (head + 1) * HEAD_DIM)
        query = q[:, at]
        old = lax.dot_general(
            query, cached[:, at], contract_last, preferred_element_type=jnp.float32
        )
        new = lax.dot_general(query, k[:, at], contract_last, preferred_element_type=jnp.float32)
        old = jnp.where(on_cached, old * scale, MASKED)
        new = jnp.where(on_fresh, new * scale, MASKED)
        top = jnp.maximum(
            jnp.max(old, axis=-1, keepdims=True), jnp.max(new, axis=-1, keepdims=True)
        )
        old = jnp.exp(old - top)
        new = jnp.exp(new - top)
        share = 1.0 / (jnp.sum(old, axis=-1, keepdims=True) + jnp.sum(new, axis=-1, keepdims=True))
        sums = jnp.dot(
            (old * share).astype(jnp.bfloat16), cached[:, after], preferred_element_type=jnp.float32
        ) + jnp.dot(
            (new * share).astype(jnp.bfloat16), v[:, at], preferred_element_type=jnp.float32
        )
        mixed[:, at] = sums.astype(jnp.bfloat16)
    load.wait()
    left = mixed[...]
    for at in range(0, weight.shape[1], TILE):
        part = jnp.dot(left, weight[:, at : at + TILE], preferred_element_type=jnp.float32)
        split_rows(part, at, outs)


def split_rows(part, at, outs):
    count = part.shape[0] // 4
    for out, block in zip(outs, (0, 2, 1, 3)):
        rows = part[block * count : (block + 1) * count]
        out[:, at : at + TILE] = rows.astype(out.dtype)


def split_shapes(rows, depth):
    return [
        jax.ShapeDtypeStruct((rows // 4, depth), kind)
        for kind in (jnp.float32, jnp.float32, jnp.bfloat16, jnp.bfloat16)
    ]


def attend(traded, q, k, v, own, came, of_row, of_column, wo):
    rows, width = q.shape
    depth = wo.shape[1]
    cached = of_column.shape[1]
    keys = cached + rows
    return pl.pallas_call(
        attend_body,
        in_specs=[smem()] + [vmem()] * 3 + [anywhere()] * 8 + [vmem()] * 2 + [anywhere()],
        out_specs=[vmem()] * 4,
        out_shape=split_shapes(rows, depth),
        scratch_shapes=[
            pltpu.VMEM((rows, width), jnp.bfloat16),
            pltpu.VMEM((cached, 2 * width), jnp.bfloat16),
            pltpu.VMEM(wo.shape, jnp.bfloat16),
            pltpu.SemaphoreType.DMA((5,)),
        ],
        compiler_params=params(),
        cost_estimate=cost(False),
    )(traded, q, k, v, *own, *came, of_row, of_column, wo)


def load_pieces(masks, info, wholes, pieces, held, sems):
    shard, width = wholes[0].shape[0], pieces[0].shape[1]
    columns = pl.ds(pl.multiple_of(info[MINE] * width, width), width)
    copies = []
    for at, mask in enumerate(masks):
        there = pl.ds(pl.multiple_of((info[WITHIN] ^ mask) * shard, shard), shard)
        for which, whole in enumerate(wholes):
            source = pieces[at - 1].at[pl.ds(which * shard, shard), :] if at else whole.at[:, columns]
            place = held.at[which, there, :]
            copies.append(pltpu.make_async_copy(source, place, sems.at[at, which]))
    for copy in copies:
        copy.start()
    return copies


def gate_up(masks, info, parts, gate, up, arrived):
    count, depth = parts[0].shape
    rows = len(parts) * count
    blocks, pieces = len(parts), len(arrived)
    width = arrived[0].shape[1]

    def body(info_ref, *refs):
        part_refs, refs = refs[:blocks], refs[blocks:]
        wholes, refs = refs[:2], refs[2:]
        piece_refs, refs = refs[:pieces], refs[pieces:]
        act_refs, (x, held, sems) = refs[:-3], refs[-3:]
        copies = load_pieces(masks, info_ref, wholes, piece_refs, held, sems)
        for at, block in enumerate(part_refs):
            x[pl.ds(at * count, count), :] = block[...]
        for copy in copies:
            copy.wait()
        for at in range(0, width, TILE):
            g = jnp.dot(x[...], held[0, :, at : at + TILE], preferred_element_type=jnp.float32)
            u = jnp.dot(x[...], held[1, :, at : at + TILE], preferred_element_type=jnp.float32)
            act = (g / (1.0 + jnp.exp(-g)) * u).astype(jnp.bfloat16)
            for group, act_ref in enumerate(act_refs):
                act_ref[:, at : at + TILE] = act[group * 4 * count : (group + 1) * 4 * count]

    return pl.pallas_call(
        body,
        in_specs=[smem()] + [vmem()] * blocks + [anywhere()] * (2 + pieces),
        out_specs=[vmem()] * (blocks // 4),
        out_shape=[jax.ShapeDtypeStruct((4 * count, width), jnp.bfloat16)] * (blocks // 4),
        scratch_shapes=[
            pltpu.VMEM((rows, depth), jnp.bfloat16),
            pltpu.VMEM((2, depth, width), jnp.bfloat16),
            pltpu.SemaphoreType.DMA((pieces + 1, 2)),
        ],
        compiler_params=params(),
        cost_estimate=cost(False),
    )(info, *parts, gate, up, *arrived)


def down_rows(masks, info, acts, down, arrived, gate=False):
    rows, width = acts[0].shape
    groups, pieces = len(acts), len(arrived)
    depth = arrived[0].shape[0] * len(masks)

    def body(info_ref, *refs):
        act_refs, down_ref, refs = refs[:groups], refs[groups], refs[groups + 1 :]
        piece_refs, outs, (held, sems) = refs[:pieces], refs[pieces:-2], refs[-2:]
        for copy in load_pieces(masks, info_ref, [down_ref], piece_refs, held, sems):
            copy.wait()
        for group, act in enumerate(act_refs):
            for at in range(0, depth, TILE):
                part = lax.dot_general(
                    act[...],
                    held[0, at : at + TILE, :],
                    (((1,), (1,)), ((), ())),
                    preferred_element_type=jnp.float32,
                )
                split_rows(part, at, outs[4 * group : 4 * group + 4])

    sums = pl.pallas_call(
        body,
        in_specs=[smem()] + [vmem()] * groups + [anywhere()] * (1 + pieces),
        out_specs=[vmem()] * (4 * groups),
        out_shape=split_shapes(rows, depth) * groups,
        scratch_shapes=[
            pltpu.VMEM((1, depth, width), jnp.bfloat16),
            pltpu.SemaphoreType.DMA((pieces + 1, 1)),
        ],
        compiler_params=params(),
        cost_estimate=cost(gate),
    )(info, *acts, down, *arrived)
    return [sums[4 * at : 4 * at + 4] for at in range(groups)]


def gather_rows(rows, across=None):
    if across is None:
        across = swap(rows, "mp", 2)
    return [rows, swap(rows, "mp", 1), across, swap(across, "mp", 1)]


def reduce_rows(own, across, far_own, far_across, edges=()):
    came = swap(far_across, "mp", 1)
    bounds = [0, *edges, own.shape[1]]
    sent = [
        (across[:, begin:end] + came[:, begin:end].astype(jnp.float32)).astype(jnp.bfloat16)
        for begin, end in zip(bounds, bounds[1:])
    ]
    other = swap(far_own, "mp", 1)
    kept = [(own[:, begin:end], other[:, begin:end]) for begin, end in zip(bounds, bounds[1:])]
    return kept, [swap(part, "mp", 2) for part in sent], sent


def total(kept, came):
    own, other = kept
    return own + other.astype(jnp.float32) + came.astype(jnp.float32)


def after(value, *earlier):
    return lax.optimization_barrier((value,) + earlier)[0] if earlier else value


def without(held, mask):
    return {at: piece for at, piece in held.items() if at != mask}


def join(*values):
    return lax.optimization_barrier(values)


def over_bits(held, bits):
    for bit in bits:
        held.update({mask ^ bit: swap(piece, "dp", bit) for mask, piece in list(held.items())})
    return held


def facts_body(info, lengths, requests, frequency, cosine, sine, of_row, of_column):
    rows = requests.shape[1]
    member, source = info[MEMBER], info[SOURCE]

    def places(size, axis, shape):
        at = lax.broadcasted_iota(jnp.int32, shape, axis)
        step = size // 4
        block = sum((at >= edge).astype(jnp.int32) for edge in (step, 2 * step, 3 * step))
        return at + ((member ^ block) - block) * step

    place = places(rows, 0, (rows, 1))
    request = requests[...]
    first, low = jnp.zeros_like(place), jnp.zeros_like(place)
    begin = lengths[source, 0]
    length = jnp.zeros_like(place) + begin
    for label in range(1, lengths.shape[1]):
        start = jnp.sum((request < label).astype(jnp.int32), axis=1, keepdims=True)
        reached = place >= start
        first = jnp.where(reached, start, first)
        low = jnp.where(reached, begin, low)
        length = jnp.where(reached, lengths[source, label], length)
        begin = begin + lengths[source, label]
    angle = (length + place - first).astype(jnp.float32) * frequency[...]
    cosine[...] = jnp.cos(angle)
    lane = lax.broadcasted_iota(jnp.int32, (1, HEAD_DIM), 1)
    sine[...] = jnp.sin(angle) * jnp.where(lane < HEAD_DIM // 2, -1.0, 1.0)
    column = lax.broadcasted_iota(jnp.int32, of_row.shape, 1)
    of_row[...] = jnp.where(
        column == 0, low, jnp.where(column == 1, low + length, jnp.where(column == 2, first, place))
    )
    of_column[0:1, :] = places(of_column.shape[1], 1, (1, of_column.shape[1]))
    of_column[1:2, :] = places(rows, 1, (1, of_column.shape[1]))


def row_facts(info, lengths, requests, cached):
    rows = requests.shape[1]
    half = HEAD_DIM // 2
    frequency = ROPE_BASE ** (-np.arange(half, dtype=np.float32) / np.float32(half))
    frequency = jnp.asarray(np.concatenate([frequency, frequency])[None], jnp.float32)
    turn = jax.ShapeDtypeStruct((rows, HEAD_DIM), jnp.float32)
    return pl.pallas_call(
        facts_body,
        in_specs=[smem(), smem(), vmem(), vmem()],
        out_specs=[vmem()] * 4,
        out_shape=[
            turn,
            turn,
            jax.ShapeDtypeStruct((rows, 8), jnp.int32),
            jax.ShapeDtypeStruct((8, cached), jnp.int32),
        ],
        compiler_params=params(),
        cost_estimate=cost(False),
    )(info, lengths, requests, frequency)


def local(
    tokens,
    request_ids,
    cache_entries,
    cached_lengths,
    traded,
    query_weight,
    key_weight,
    value_weight,
    output_weight,
    gate_weight,
    up_weight,
    down_weight,
):
    replica = lax.axis_index("rep")
    within = lax.axis_index("dp")
    member = lax.axis_index("mp")
    planes = lax.axis_size("dp")
    pair = planes // 2
    bits = [1 << at for at in range(planes.bit_length() - 1) if 1 << at != pair]
    place = (within // pair) % 2
    mine, leaving = 2 * place + replica, 2 * (1 - place) + replica
    source = jnp.where(traded[0] == 1, 1 - replica, replica) * planes + within
    info = jnp.stack([member, within, mine, leaving, source]).astype(jnp.int32)

    *normed, blocks_0, blocks_1, blocks_2, blocks_3, wide_leaving, wide_mine = prepare(
        info, tokens, cache_entries, gate_weight, up_weight
    )
    blocks = [blocks_0, swap(blocks_1, "mp", 1), swap(blocks_2, "mp", 2), swap(blocks_3, "mp", 3)]
    facts = row_facts(info, cached_lengths, request_ids, 4 * cache_entries.shape[0])
    came = [swap(block, "rep", 1) for block in blocks]
    over_chip = [swap(half, "mp", 2) for half in normed]
    over_chip, came[0], came[1] = join(over_chip, came[0], came[1])
    parts = [gather_rows(*halves) for halves in zip(normed, over_chip)]
    parts = [half for pair_of in zip(*parts) for half in pair_of]

    def near_side(piece):
        return without(over_bits({0: piece}, bits), 0)

    def across(piece):
        return {pair: swap(piece, "dp", pair)}

    def far_side(held):
        return without(over_bits(dict(held), bits), pair)

    wide = {**across(wide_leaving), **near_side(after(wide_mine, blocks[1]))}

    q, k, v = project(parts, facts[0], facts[1], query_weight, key_weight, value_weight)
    came, q = join(came, q)
    sums = attend(traded, q, k, v, blocks, came, facts[2], facts[3], output_weight)
    sums, wide = join(sums, wide)
    (kept,), (came,), (sent,) = reduce_rows(*sums)
    down_cut = cut(info, after(down_weight, sent))
    kept, came, down_cut = join(kept, came, down_cut)
    wide.update(far_side({pair: wide[pair]}))
    state_own = (tokens.astype(jnp.float32) + total(kept, came)).astype(jnp.bfloat16)
    normed_own = layer_norm(state_own.astype(jnp.float32)).astype(jnp.bfloat16)

    rows_z = swap(normed_own, "dp", pair)
    rows_x = swap(normed_own, "rep", 1)
    over_chip = swap(normed_own, "mp", 2), swap(rows_x, "mp", 2)
    rows_z, wide, over_chip = join(rows_z, wide, over_chip)
    parts = gather_rows(normed_own, over_chip[0]) + gather_rows(rows_x, over_chip[1])
    rows_both = swap(rows_z, "rep", 1)
    rows_z = gather_rows(rows_z)
    back = {**across(after(down_cut[0], rows_x)), **near_side(after(down_cut[1], rows_z[1]))}
    parts += rows_z
    masks = [0] + list(wide)
    in_order = lambda held: [held[mask] for mask in masks[1:]]
    acts = gate_up(masks, info, parts, gate_weight, up_weight, in_order(wide))
    parts = gather_rows(rows_both)
    parts[0] = after(parts[0], acts[0])
    acts, back = join(acts, back)
    back.update(far_side({pair: back[pair]}))
    acts += gate_up(masks, info, parts, gate_weight, up_weight, in_order(wide))

    def sums_of(*groups, gate=False):
        return down_rows(masks, info, groups, down_weight, in_order(back), gate)

    def crossed(value, axis, mask):
        return swap(value.astype(jnp.bfloat16), axis, mask).astype(jnp.float32)

    edges = (tokens.shape[1] * 5 // 8,)
    found_both, found_z = sums_of(acts[3], acts[2])
    kept, came, sent = reduce_rows(*found_both, edges)
    kept_z, came_z, sent_z = reduce_rows(*found_z, edges)
    found_x, found = sums_of(after(acts[1], *sent, *sent_z), acts[0], gate=True)
    came[0], came_z[0], found_x, found = join(came[0], came_z[0], found_x, found)
    of_both = [total(*terms).astype(jnp.bfloat16) for terms in zip(kept, came)]
    of_z = [total(*terms) for terms in zip(kept_z, came_z)]
    sent = [
        (part + crossed(more, "rep", 1)).astype(jnp.bfloat16) for part, more in zip(of_z, of_both)
    ]
    of_z = jnp.concatenate([swap(part, "dp", pair) for part in sent], axis=1).astype(jnp.float32)
    found_x, found = after((found_x, found), *of_both)
    (kept,), (came,), sent_x = reduce_rows(*found_x)
    of_x = total(kept, came)
    (kept,), (came,), _ = reduce_rows(*after(found, *sent_x))
    of_own = total(kept, came)
    of_x = after(of_x, *sent)
    columns = of_x.shape[1]
    of_x = [crossed(of_x[:, at : at + columns // 2], "rep", 1) for at in (0, columns // 2)]
    of_own = of_own + jnp.concatenate(of_x, axis=1)
    return (state_own.astype(jnp.float32) + (of_own + of_z)).astype(jnp.bfloat16)


def solution(mesh):
    in_specs = (
        P(("rep", "dp", "mp"), None),
        P(("rep", "dp"), None),
        P(("rep", "dp", "mp"), None),
        P(),
        P("dp"),
        P(None, "mp"),
        P(None, "mp"),
        P(None, "mp"),
        P("mp", None),
        P("dp", "mp"),
        P("dp", "mp"),
        P("dp", "mp"),
    )
    out_specs = P(("rep", "dp", "mp"), None)
    return jax.shard_map(local, mesh=mesh, in_specs=in_specs, out_specs=out_specs, check_vma=False)
```
